32 devices in a mesh: row: 4 (over z), col: 8 (over y, x, core).
Axes of the slice: x: 2, y: 2, z: 4, core: 2. Of those that a mesh axis runs over, the one named last changes fastest.
Arguments:
- amplitudes: float32 [4096, 4096], P('row', 'col'), may hold values from -1 to 1, as said below
- factors: float32 [4096, 256], P('row', 'col'), may hold values from -1.5 to 1.5
- occ_index: int32 [4096], replicated, may hold values from 0 to 63
- vir_index: int32 [4096], replicated, may hold values from 0 to 2047
- occ_energy: float32 [64], replicated, may hold values from -3 to -0.5
- vir_energy: float32 [2048], replicated, may hold values from 0.2 to 3
Outputs:
- new_amplitudes: float32 [4096, 4096], P('row', 'col')
The draws below stay inside these ranges and needn't reach their ends.
Inputs may be any that keep to these rules, and one draw needn't show every extreme that they name: amplitudes is symmetric: amplitudes[p, q] equals amplitudes[q, p].
All inputs are finite; a program needn't handle non-finite values.
Results may differ from the reference program's by a relative error of at most 0.000096.
Values sent between devices are 32-bit elements; how exact they have to be, the bound alone decides.
No kernel may reach another device: no remote copies, remote signals or barrier semaphores. Data moves between devices by JAX's collectives and lax.ppermute only.
A program may use at most 64 MiB of HBM per device.

```python
import jax
import jax.numpy as jnp
from jax import lax

K = 256
NOCC = 64
NVIR = 2048
P_SIZE = 4096
N_ROW = 4


def draw_amplitudes(key, part):
    raw_normal = jnp.clip(jax.random.normal(key, (P_SIZE, P_SIZE), jnp.float32), -6.0, 6.0)
    symmetric = 0.5 * (raw_normal + raw_normal.T)
    return jnp.clip(symmetric / jnp.sqrt(jnp.float32(P_SIZE)), -1.0, 1.0)


def set_ends(array, stream_key, low, high):
    index_at = [jax.random.randint(jax.random.fold_in(stream_key, axis), (), 0, length) for axis, length in enumerate(array.shape)]
    widest = array.shape.index(max(array.shape))
    beside = index_at[:widest] + [(index_at[widest] + 1) % array.shape[widest]] + index_at[widest + 1:]
    return array.at[tuple(index_at)].set(low).at[tuple(beside)].set(high)


def shard_levels(key, extent, cuts, low, high):
    level, own = 1.0, jax.random.fold_in(key, 6)
    for position, parts in cuts:
        heights = jnp.exp(jax.random.uniform(jax.random.fold_in(own, position), (parts,), jnp.float32, low / len(cuts), high / len(cuts)))
        level = level * jnp.repeat(heights, extent[position] // parts).reshape([-1 if axis == position else 1 for axis in range(len(extent))])
    return level


def scatter_about(own_key, extent, spread, limit, shards=(), kind=jnp.bfloat16):
    entries = spread * jax.random.normal(own_key, extent, jnp.float32)
    if shards:
        entries = entries * shard_levels(own_key, extent, shards, -0.22, 0.18)
    return jnp.clip(entries, -limit, limit).astype(kind)


def setup_inputs(seed: int = 0) -> dict:
    seeds = jax.random.split(jax.random.key(seed), 7)
    amplitudes = draw_amplitudes(jax.random.fold_in(seeds[6], 71), 0)
    factors = scatter_about(seeds[1], (P_SIZE, K), 0.25, 1.5, ((0, 4), (1, 8)), jnp.float32)
    occ_index = set_ends(jax.random.randint(seeds[2], (P_SIZE,), 0, NOCC), jax.random.fold_in(seeds[2], 1), 0, NOCC - 1).astype(jnp.int32)
    vir_index = set_ends(jax.random.randint(seeds[3], (P_SIZE,), 0, NVIR), jax.random.fold_in(seeds[3], 1), 0, NVIR - 1).astype(jnp.int32)
    occ_energy = jnp.clip(jax.random.uniform(seeds[4], (NOCC,), jnp.float32, -3.0, -0.5), -3.0, -0.5)
    vir_energy = jnp.clip(jax.random.uniform(seeds[5], (NVIR,), jnp.float32, 0.2, 3.0), 0.2, 3.0)
    return dict(amplitudes=amplitudes, factors=factors, occ_index=occ_index, vir_index=vir_index, occ_energy=occ_energy, vir_energy=vir_energy)


def pair_energy(occ_index, vir_index, occ_energy, vir_energy):
    return vir_energy[vir_index] - occ_energy[occ_index]


def reference(amplitudes, factors, occ_index, vir_index, occ_energy, vir_energy):
    energy = pair_energy(occ_index, vir_index, occ_energy, vir_energy)
    product = jnp.dot(amplitudes, factors, precision=lax.Precision.HIGHEST, preferred_element_type=jnp.float32)
    dressed = factors + product
    row_blocks = dressed.reshape(N_ROW, P_SIZE // N_ROW, K)
    energy_blocks = energy.reshape(N_ROW, P_SIZE // N_ROW)

    def outer_block(items):
        row_block, row_energy = items
        contracted = lax.dot_general(row_block, dressed, (((1,), (1,)), ((), ())), precision=lax.Precision.HIGHEST, preferred_element_type=jnp.float32)
        return -contracted / (row_energy[:, None] + energy[None, :])

    stacked = lax.map(outer_block, (row_blocks, energy_blocks))
    return stacked.reshape(P_SIZE, P_SIZE)
```

```python
import functools

import jax
import jax.numpy as jnp
from jax import lax
from jax.experimental import pallas as pl
from jax.experimental.pallas import tpu as pltpu
from jax.sharding import PartitionSpec as P

AXES = ("row", "col")
MIB = 1 << 20


def split(x):
    high = x.astype(jnp.bfloat16)
    low = (x - high.astype(jnp.float32)).astype(jnp.bfloat16)
    return high, low


def params(*arrays):
    held = sum(a.size * a.dtype.itemsize for a in arrays)
    return pltpu.CompilerParams(vmem_limit_bytes=2 * held + 4 * MIB)


def whole_specs(count):
    return [pl.BlockSpec(memory_space=pltpu.VMEM)] * count


def shape_of(shape, dtype=jnp.float32):
    return jax.ShapeDtypeStruct(shape, dtype)


def prepare_kernel(place, own_ref, sibling_ref, high_ref, low_ref):
    half = sibling_ref.shape[0]
    wide = own_ref.shape[1]
    core = place[0]
    own = own_ref[pl.ds(pl.multiple_of(core * half, half), half), :].T
    high, low = split(own)
    here = pl.ds(pl.multiple_of(core * wide, wide), wide)
    high_ref[here, :] = high
    low_ref[here, :] = low
    high, low = split(sibling_ref[...].T)
    there = pl.ds(pl.multiple_of((1 - core) * wide, wide), wide)
    high_ref[there, :] = high
    low_ref[there, :] = low


def prepare(core, own, sibling):
    half, wide = sibling.shape
    out = shape_of((2 * wide, half), jnp.bfloat16)
    return pl.pallas_call(
        prepare_kernel,
        out_shape=(out, out),
        in_specs=[pl.BlockSpec(memory_space=pltpu.SMEM)] + whole_specs(2),
        out_specs=whole_specs(2),
        compiler_params=params(own, sibling, out, out),
        cost_estimate=pl.CostEstimate(flops=0, bytes_accessed=own.size * 12, transcendentals=0),
        name="prepare",
    )(core.reshape(1), own, sibling)


def contract_kernel(own_ref, sibling_ref, high_ref, low_ref, out_ref):
    factors = jnp.concatenate([own_ref[...], sibling_ref[...]], axis=0)
    rows = factors.shape[0]
    high, low = split(factors)
    both = jnp.concatenate([high, low], axis=0)
    first = jnp.dot(both, high_ref[...], preferred_element_type=jnp.float32)
    second = jnp.dot(high, low_ref[...], preferred_element_type=jnp.float32)
    out_ref[...] = first[:rows] + (first[rows:] + second)


def contract(own, sibling, high, low):
    out = shape_of((2 * own.shape[0], high.shape[1]))
    return pl.pallas_call(
        contract_kernel,
        out_shape=out,
        in_specs=whole_specs(4),
        out_specs=whole_specs(1)[0],
        compiler_params=params(own, sibling, high, low, out),
        cost_estimate=pl.CostEstimate(
            flops=6 * out.size * high.shape[0], bytes_accessed=high.size * 4, transcendentals=0
        ),
        name="contract",
    )(own, sibling, high, low)


def pick(table, index):
    rows, lanes = table.shape
    length = index.shape[1]
    at_lane = lax.broadcasted_iota(jnp.int32, (lanes, length), 0) == index % lanes
    picked = jnp.dot(
        table,
        at_lane.astype(jnp.float32),
        precision=lax.Precision.HIGHEST,
        preferred_element_type=jnp.float32,
    )
    at_row = lax.broadcasted_iota(jnp.int32, (rows, length), 0) == index // lanes
    return jnp.sum(jnp.where(at_row, picked, 0.0), axis=0, keepdims=True)


def energy_kernel(place, occ_ref, vir_ref, occ_table, vir_table, rows_ref, cols_ref):
    for number, out_ref in enumerate((rows_ref, cols_ref)):
        length = out_ref.shape[1]
        here = pl.ds(pl.multiple_of(place[number] * length, length), length)
        out_ref[...] = pick(vir_table[...], vir_ref[:, here]) - pick(occ_table[...], occ_ref[:, here])


def as_table(energies):
    lanes = 128
    padded = jnp.pad(energies, (0, -energies.shape[0] % lanes))
    return padded.reshape(-1, lanes)


def pair_energies(place, occ_index, vir_index, occ_energy, vir_energy, rows, cols):
    occ_index, vir_index = occ_index[None, :], vir_index[None, :]
    occ_table, vir_table = as_table(occ_energy), as_table(vir_energy)
    return pl.pallas_call(
        energy_kernel,
        out_shape=(shape_of((1, rows)), shape_of((1, cols))),
        in_specs=[pl.BlockSpec(memory_space=pltpu.SMEM)] + whole_specs(4),
        out_specs=whole_specs(2),
        compiler_params=pltpu.CompilerParams(vmem_limit_bytes=8 * MIB),
        cost_estimate=pl.CostEstimate(flops=0, bytes_accessed=MIB, transcendentals=0),
        name="energies",
    )(place, occ_index, vir_index, occ_table, vir_table)


def outer_kernel(slots, place, rows_energy, cols_energy, *refs):
    own, other, columns = refs[:slots], refs[slots : 2 * slots], refs[2 * slots : 3 * slots]
    out_ref, high_ref, low_ref = refs[3 * slots :]
    step, steps = pl.program_id(0), pl.num_programs(0)
    depth, wide = columns[0].shape
    tall = out_ref.shape[0]

    @pl.when(step == 0)
    def _():
        for slot in range(slots):
            high, low = split(columns[slot][...])
            high_ref[pl.ds(slot * depth, depth), :] = high
            low_ref[pl.ds(slot * depth, depth), :] = low

    def finish(left, number):
        left = left.T
        high, low = split(left)
        total = jnp.dot(low, high_ref[...], preferred_element_type=jnp.float32)
        total += jnp.dot(high, low_ref[...], preferred_element_type=jnp.float32)
        total += jnp.dot(high, high_ref[...], preferred_element_type=jnp.float32)
        at = pl.ds(pl.multiple_of(number * tall, tall), tall)
        row = jnp.broadcast_to(rows_energy[:, at], (128, tall)).T
        denominator = jnp.concatenate([row] * (wide // 128), axis=1) + cols_energy[...]
        out_ref[...] = -total / denominator

    per_half = steps // 2
    inner = step % per_half
    here = pl.ds(pl.multiple_of(inner * tall, tall), tall)
    core = place[0]

    @pl.when(step < per_half)
    def _():
        finish(jnp.concatenate([ref[:, here] for ref in own], axis=0), core * per_half + inner)

    @pl.when(step >= per_half)
    def _():
        half = depth // 2
        parts = []
        for ref in other:
            parts += [ref[half:, here], ref[:half, here]]
        finish(jnp.concatenate(parts, axis=0), (1 - core) * per_half + inner)


def outer(core, rows_energy, cols_energy, own, other, columns):
    slots = len(own)
    depth, wide = columns[0].shape
    half = own[0].shape[1]
    tall = min(256, half)
    per_half = half // tall

    def place_of(step, place):
        number = jnp.where(step < per_half, place[0], 1 - place[0]) * per_half + step % per_half
        return number, 0

    arrays = [*own, *other, *columns]
    out = shape_of((2 * half, wide))
    parts = pltpu.VMEM((slots * depth, wide), jnp.bfloat16)
    return pl.pallas_call(
        functools.partial(outer_kernel, slots),
        out_shape=out,
        grid_spec=pltpu.PrefetchScalarGridSpec(
            num_scalar_prefetch=1,
            grid=(2 * per_half,),
            in_specs=whole_specs(2 + len(arrays)),
            out_specs=pl.BlockSpec((tall, wide), place_of),
            scratch_shapes=[parts, parts],
        ),
        compiler_params=pltpu.CompilerParams(
            vmem_limit_bytes=sum(a.size * 4 for a in arrays) + 10 * tall * wide * 4 + 8 * MIB
        ),
        cost_estimate=pl.CostEstimate(
            flops=6 * out.size * slots * depth, bytes_accessed=out.size * 4, transcendentals=0
        ),
        name="outer",
    )(core.reshape(1), rows_energy, cols_energy, *arrays)


def local(rows, cols, amplitudes, factors, occ_index, vir_index, occ_energy, vir_energy):
    cores = cols // rows
    chips = [(z, j, s) for z in range(rows) for j in range(rows) for s in range(cores)]

    def number(z, j, s):
        return z * cols + j * cores + s

    def move(x, to):
        return lax.ppermute(x, AXES, [(number(*at), number(*to(*at))) for at in chips])

    def swap(x):
        return move(x, lambda z, j, s: (z, j, 1 - s))

    def transposed(x, t):
        return move(x, lambda z, j, s: (j ^ z ^ t, z, s))

    def across(x, t):
        return move(x, lambda z, j, s: (z, z ^ j ^ t, s))

    slots = range(rows)
    col_index = lax.axis_index("col")
    row_index = lax.axis_index("row")
    core = col_index % cores
    tall, wide = amplitudes.shape
    half = tall // cores
    pieces = factors.T

    received = [transposed(pieces, t) for t in slots]
    for_sibling = lax.dynamic_slice_in_dim(amplitudes, (1 - core) * half, half, 0)
    high, low = prepare(core, amplitudes, swap(for_sibling))
    place = jnp.stack([row_index, col_index]).astype(jnp.int32)
    rows_energy, cols_energy = pair_energies(
        place, occ_index, vir_index, occ_energy, vir_energy, tall, wide
    )
    both = jnp.concatenate([pieces, swap(pieces)], axis=0)
    total = lax.dynamic_slice_in_dim(both, core * half, half, 1)
    for t in slots:
        partial = contract(received[t], swap(received[t]), high, low)
        total = total + across(partial, t)
    columns = [transposed(total, t) for t in slots]
    own = [across(total, t) for t in slots]
    other = [swap(x) for x in own]
    return outer(core, rows_energy, cols_energy, own, other, columns)


def solution(mesh):
    rows, cols = mesh.shape["row"], mesh.shape["col"]
    return jax.shard_map(
        functools.partial(local, rows, cols),
        mesh=mesh,
        in_specs=(P("row", "col"), P("row", "col"), P(), P(), P(), P()),
        out_specs=P("row", "col"),
        check_vma=False,
    )
```

```python
import functools

import jax
import jax.numpy as jnp
from jax import lax
from jax.experimental import pallas as pl
from jax.experimental.pallas import tpu as pltpu
from jax.sharding import PartitionSpec as P

AXES = ("row", "col")
MIB = 1 << 20


def split(x):
    high = x.astype(jnp.bfloat16)
    low = (x - high.astype(jnp.float32)).astype(jnp.bfloat16)
    return high, low


def params(*arrays):
    held = sum(a.size * a.dtype.itemsize for a in arrays)
    return pltpu.CompilerParams(vmem_limit_bytes=2 * held + 4 * MIB)


def whole_specs(count):
    return [pl.BlockSpec(memory_space=pltpu.VMEM)] * count


def shape_of(shape, dtype=jnp.float32):
    return jax.ShapeDtypeStruct(shape, dtype)


def prepare_kernel(place, own_ref, sibling_ref, high_ref, low_ref):
    wide = own_ref.shape[1]
    core = place[0]
    for number, ref in ((core, own_ref), (1 - core, sibling_ref)):
        high, low = split(ref[...].T)
        here = pl.ds(pl.multiple_of(number * wide, wide), wide)
        high_ref[here, :] = high
        low_ref[here, :] = low


def prepare(core, own, sibling):
    tall, wide = own.shape
    out = shape_of((2 * wide, tall), jnp.bfloat16)
    return pl.pallas_call(
        prepare_kernel,
        out_shape=(out, out),
        in_specs=[pl.BlockSpec(memory_space=pltpu.SMEM)] + whole_specs(2),
        out_specs=whole_specs(2),
        compiler_params=params(own, sibling, out, out),
        cost_estimate=pl.CostEstimate(flops=0, bytes_accessed=own.size * 16, transcendentals=0),
        name="prepare",
    )(core.reshape(1), own, sibling)


def contract_kernel(factors_ref, high_ref, low_ref, out_ref):
    rows = factors_ref.shape[0]
    high, low = split(factors_ref[...])
    both = jnp.concatenate([high, low], axis=0)
    first = jnp.dot(both, high_ref[...], preferred_element_type=jnp.float32)
    second = jnp.dot(high, low_ref[...], preferred_element_type=jnp.float32)
    out_ref[...] = first[:rows] + (first[rows:] + second)


def contract(factors, high, low):
    out = shape_of((factors.shape[0], high.shape[1]))
    return pl.pallas_call(
        contract_kernel,
        out_shape=out,
        in_specs=whole_specs(3),
        out_specs=whole_specs(1)[0],
        compiler_params=params(factors, high, low, out),
        cost_estimate=pl.CostEstimate(
            flops=6 * out.size * high.shape[0], bytes_accessed=high.size * 4, transcendentals=0
        ),
        name="contract",
    )(factors, high, low)


def pick(table, index):
    rows, lanes = table.shape
    length = index.shape[1]
    at_lane = lax.broadcasted_iota(jnp.int32, (lanes, length), 0) == index % lanes
    picked = jnp.dot(
        table,
        at_lane.astype(jnp.float32),
        precision=lax.Precision.HIGHEST,
        preferred_element_type=jnp.float32,
    )
    at_row = lax.broadcasted_iota(jnp.int32, (rows, length), 0) == index // lanes
    return jnp.sum(jnp.where(at_row, picked, 0.0), axis=0, keepdims=True)


def energy_kernel(place, occ_ref, vir_ref, occ_table, vir_table, rows_ref, cols_ref):
    for number, out_ref in enumerate((rows_ref, cols_ref)):
        length = out_ref.shape[1]
        here = pl.ds(pl.multiple_of(place[number] * length, length), length)
        out_ref[...] = pick(vir_table[...], vir_ref[:, here]) - pick(occ_table[...], occ_ref[:, here])


def as_table(energies):
    lanes = 128
    padded = jnp.pad(energies, (0, -energies.shape[0] % lanes))
    return padded.reshape(-1, lanes)


def pair_energies(place, occ_index, vir_index, occ_energy, vir_energy, rows, cols):
    occ_index, vir_index = occ_index[None, :], vir_index[None, :]
    occ_table, vir_table = as_table(occ_energy), as_table(vir_energy)
    return pl.pallas_call(
        energy_kernel,
        out_shape=(shape_of((1, rows)), shape_of((1, cols))),
        in_specs=[pl.BlockSpec(memory_space=pltpu.SMEM)] + whole_specs(4),
        out_specs=whole_specs(2),
        compiler_params=pltpu.CompilerParams(vmem_limit_bytes=8 * MIB),
        cost_estimate=pl.CostEstimate(flops=0, bytes_accessed=MIB, transcendentals=0),
        name="energies",
    )(place, occ_index, vir_index, occ_table, vir_table)


def outer_kernel(slots, place, rows_energy, cols_energy, *refs):
    left, right = refs[:slots], refs[slots : 2 * slots]
    out_ref, left_ref, high_ref, low_ref = refs[2 * slots :]
    step = pl.program_id(0)
    depth = left[0].shape[0]
    tall, wide = out_ref.shape

    @pl.when(step == 0)
    def _():
        mine = pl.ds(pl.multiple_of(place[0] * wide, wide), wide)
        for slot in range(slots):
            left_ref[pl.ds(pl.multiple_of(place[1 + slot] * depth, depth), depth), :] = left[slot][...]
            high, low = split(right[slot][:, mine])
            here = pl.ds(pl.multiple_of(place[1 + slots + slot] * depth, depth), depth)
            high_ref[here, :] = high
            low_ref[here, :] = low

    here = pl.ds(pl.multiple_of(step * tall, tall), tall)
    high, low = split(left_ref[:, here].T)
    total = jnp.dot(low, high_ref[...], preferred_element_type=jnp.float32)
    total += jnp.dot(high, low_ref[...], preferred_element_type=jnp.float32)
    total += jnp.dot(high, high_ref[...], preferred_element_type=jnp.float32)
    row = jnp.broadcast_to(rows_energy[:, here], (128, tall)).T
    denominator = jnp.concatenate([row] * (wide // 128), axis=1) + cols_energy[...]
    out_ref[...] = -total / denominator


def outer(place, rows_energy, cols_energy, left, right):
    slots = len(left)
    depth, total = left[0].shape
    wide = cols_energy.shape[1]
    tall = min(256, total)
    arrays = [*left, *right]
    out = shape_of((total, wide))
    parts = pltpu.VMEM((slots * depth, wide), jnp.bfloat16)
    return pl.pallas_call(
        functools.partial(outer_kernel, slots),
        out_shape=out,
        grid_spec=pltpu.PrefetchScalarGridSpec(
            num_scalar_prefetch=1,
            grid=(total // tall,),
            in_specs=whole_specs(2 + len(arrays)),
            out_specs=pl.BlockSpec((tall, wide), lambda step, place: (step, 0)),
            scratch_shapes=[pltpu.VMEM((slots * depth, total), jnp.float32), parts, parts],
        ),
        compiler_params=pltpu.CompilerParams(
            vmem_limit_bytes=sum(a.size * 4 for a in arrays) * 2 + 10 * tall * wide * 4 + 8 * MIB
        ),
        cost_estimate=pl.CostEstimate(
            flops=6 * out.size * slots * depth, bytes_accessed=out.size * 4, transcendentals=0
        ),
        name="outer",
    )(place, rows_energy, cols_energy, *arrays)


def local(rows, cols, amplitudes, factors, occ_index, vir_index, occ_energy, vir_energy):
    cores = 2
    share = rows // cores
    chips = [(z, j, s) for z in range(rows) for j in range(rows) for s in range(cores)]

    def number(z, j, s):
        return z * cols + j * cores + s

    def move(x, to):
        return lax.ppermute(x, AXES, [(number(*at), number(*to(*at))) for at in chips])

    def swap(x):
        return move(x, lambda z, j, s: (z, j, 1 - s))

    def transposed(x, i):
        return move(x, lambda z, j, s: (j ^ z ^ (s * share + i), z, s))

    def reduced(x, i):
        return move(x, lambda z, j, s: (z, z ^ j ^ (s * share + i), s))

    def across(x, i):
        return move(x, lambda z, j, s: (z, j ^ (s * share + i), s))

    turns = range(share)
    row_index = lax.axis_index("row").astype(jnp.int32)
    col_index = lax.axis_index("col").astype(jnp.int32)
    core, chip = col_index % cores, col_index // cores
    tall, wide = amplitudes.shape

    def share_of(x):
        other = swap(x)
        return jnp.where(
            core == 0, jnp.concatenate([x, other], axis=0), jnp.concatenate([other, x], axis=0)
        )

    pieces = share_of(factors.T)
    received = [transposed(pieces, i) for i in turns]
    high, low = prepare(core, amplitudes, swap(amplitudes))
    rows_energy, cols_energy = pair_energies(
        jnp.stack([row_index, col_index]), occ_index, vir_index, occ_energy, vir_energy, tall, wide
    )
    high, low, rows_energy, cols_energy = lax.optimization_barrier(
        (high, low, rows_energy, cols_energy)
    )
    arrived = [reduced(contract(received[i], high, low), i) for i in turns]
    total = functools.reduce(jnp.add, arrived)
    dressed = pieces + (total + swap(total))
    columns = [transposed(dressed, i) for i in turns]
    own = [across(dressed, i) for i in turns]
    columns += [swap(x) for x in columns]
    own += [swap(x) for x in own]
    turn = jnp.concatenate([core * share + jnp.arange(share), (1 - core) * share + jnp.arange(share)])
    place = jnp.concatenate([core[None], chip ^ turn, row_index ^ chip ^ turn]).astype(jnp.int32)
    return outer(place, rows_energy, cols_energy, own, columns)


def solution(mesh):
    rows, cols = mesh.shape["row"], mesh.shape["col"]
    return jax.shard_map(
        functools.partial(local, rows, cols),
        mesh=mesh,
        in_specs=(P("row", "col"), P("row", "col"), P(), P(), P(), P()),
        out_specs=P("row", "col"),
        check_vma=False,
    )
```

```python
import functools

import jax
import jax.numpy as jnp
from jax import lax
from jax.experimental import pallas as pl
from jax.experimental.pallas import tpu as pltpu
from jax.sharding import PartitionSpec as P

AXES = ("row", "col")
MIB = 1 << 20


def split(x):
    high = x.astype(jnp.bfloat16)
    low = (x - high.astype(jnp.float32)).astype(jnp.bfloat16)
    return high, low


def params(*arrays):
    held = sum(a.size * a.dtype.itemsize for a in arrays)
    return pltpu.CompilerParams(vmem_limit_bytes=2 * held + 4 * MIB)


def whole_specs(count):
    return [pl.BlockSpec(memory_space=pltpu.VMEM)] * count


def shape_of(shape, dtype=jnp.float32):
    return jax.ShapeDtypeStruct(shape, dtype)


def prepare_kernel(place, own_ref, sibling_ref, high_ref, low_ref):
    wide = own_ref.shape[1]
    core = place[0]
    for number, ref in ((core, own_ref), (1 - core, sibling_ref)):
        high, low = split(ref[...].T)
        here = pl.ds(pl.multiple_of(number * wide, wide), wide)
        high_ref[here, :] = high
        low_ref[here, :] = low


def prepare(core, own, sibling):
    tall, wide = own.shape
    out = shape_of((2 * wide, tall), jnp.bfloat16)
    return pl.pallas_call(
        prepare_kernel,
        out_shape=(out, out),
        in_specs=[pl.BlockSpec(memory_space=pltpu.SMEM)] + whole_specs(2),
        out_specs=whole_specs(2),
        compiler_params=params(own, sibling, out, out),
        cost_estimate=pl.CostEstimate(flops=0, bytes_accessed=own.size * 16, transcendentals=0),
        name="prepare",
    )(core.reshape(1), own, sibling)


def contract_kernel(factors_ref, high_ref, low_ref, out_ref):
    rows = factors_ref.shape[0]
    high, low = split(factors_ref[...])
    both = jnp.concatenate([high, low], axis=0)
    first = jnp.dot(both, high_ref[...], preferred_element_type=jnp.float32)
    second = jnp.dot(high, low_ref[...], preferred_element_type=jnp.float32)
    out_ref[...] = first[:rows] + (first[rows:] + second)


def contract(factors, high, low):
    out = shape_of((factors.shape[0], high.shape[1]))
    return pl.pallas_call(
        contract_kernel,
        out_shape=out,
        in_specs=whole_specs(3),
        out_specs=whole_specs(1)[0],
        compiler_params=params(factors, high, low, out),
        cost_estimate=pl.CostEstimate(
            flops=6 * out.size * high.shape[0], bytes_accessed=high.size * 4, transcendentals=0
        ),
        name="contract",
    )(factors, high, low)


def pick(table, index):
    rows, lanes = table.shape
    length = index.shape[1]
    at_lane = lax.broadcasted_iota(jnp.int32, (lanes, length), 0) == index % lanes
    picked = jnp.dot(
        table,
        at_lane.astype(jnp.float32),
        precision=lax.Precision.HIGHEST,
        preferred_element_type=jnp.float32,
    )
    at_row = lax.broadcasted_iota(jnp.int32, (rows, length), 0) == index // lanes
    return jnp.sum(jnp.where(at_row, picked, 0.0), axis=0, keepdims=True)


def energy_kernel(place, occ_ref, vir_ref, occ_table, vir_table, rows_ref, cols_ref):
    for number, out_ref in enumerate((rows_ref, cols_ref)):
        length = out_ref.shape[1]
        here = pl.ds(pl.multiple_of(place[number] * length, length), length)
        out_ref[...] = pick(vir_table[...], vir_ref[:, here]) - pick(occ_table[...], occ_ref[:, here])


def as_table(energies):
    lanes = 128
    padded = jnp.pad(energies, (0, -energies.shape[0] % lanes))
    return padded.reshape(-1, lanes)


def pair_energies(place, occ_index, vir_index, occ_energy, vir_energy, rows, cols):
    occ_index, vir_index = occ_index[None, :], vir_index[None, :]
    occ_table, vir_table = as_table(occ_energy), as_table(vir_energy)
    return pl.pallas_call(
        energy_kernel,
        out_shape=(shape_of((1, rows)), shape_of((1, cols))),
        in_specs=[pl.BlockSpec(memory_space=pltpu.SMEM)] + whole_specs(4),
        out_specs=whole_specs(2),
        compiler_params=pltpu.CompilerParams(vmem_limit_bytes=8 * MIB),
        cost_estimate=pl.CostEstimate(flops=0, bytes_accessed=MIB, transcendentals=0),
        name="energies",
    )(place, occ_index, vir_index, occ_table, vir_table)


def left_kernel(slots, *refs):
    high_ref, low_ref = refs[slots:]
    depth = refs[0].shape[0]
    step = 128 // depth
    for slot in range(0, slots, step):
        block = jnp.concatenate([refs[slot + k][...] for k in range(step)], axis=0).T
        high, low = split(block)
        here = pl.ds(slot * depth, step * depth)
        high_ref[:, here] = high
        low_ref[:, here] = low


def left_parts(left):
    slots = len(left)
    depth, total = left[0].shape
    out = shape_of((total, slots * depth), jnp.bfloat16)
    return pl.pallas_call(
        functools.partial(left_kernel, slots),
        out_shape=(out, out),
        in_specs=whole_specs(slots),
        out_specs=whole_specs(2),
        compiler_params=params(*left, out, out),
        cost_estimate=pl.CostEstimate(flops=0, bytes_accessed=out.size * 8, transcendentals=0),
        name="left_parts",
    )(*left)


def outer_kernel(slots, place, rows_energy, cols_energy, left_high, left_low, *refs):
    right = refs[:slots]
    out_ref, high_ref, low_ref = refs[slots:]
    step = pl.program_id(0)
    depth = right[0].shape[0]
    tall, wide = out_ref.shape

    @pl.when(step == 0)
    def _():
        mine = pl.ds(pl.multiple_of(place[0] * wide, wide), wide)
        for slot in range(slots):
            high, low = split(right[slot][:, mine])
            here = pl.ds(pl.multiple_of(place[1 + slot] * depth, depth), depth)
            high_ref[here, :] = high
            low_ref[here, :] = low

    here = pl.ds(pl.multiple_of(step * tall, tall), tall)
    high, low = left_high[here, :], left_low[here, :]
    total = jnp.dot(low, high_ref[...], preferred_element_type=jnp.float32)
    total += jnp.dot(high, low_ref[...], preferred_element_type=jnp.float32)
    total += jnp.dot(high, high_ref[...], preferred_element_type=jnp.float32)
    row = jnp.broadcast_to(rows_energy[:, here], (128, tall)).T
    denominator = jnp.concatenate([row] * (wide // 128), axis=1) + cols_energy[...]
    out_ref[...] = -total / denominator


def outer(place, rows_energy, cols_energy, left_high, left_low, right):
    slots = len(right)
    depth, total = right[0].shape
    wide = cols_energy.shape[1]
    tall = min(256, total)
    arrays = [left_high, left_low, *right]
    out = shape_of((total, wide))
    parts = pltpu.VMEM((slots * depth, wide), jnp.bfloat16)
    return pl.pallas_call(
        functools.partial(outer_kernel, slots),
        out_shape=out,
        grid_spec=pltpu.PrefetchScalarGridSpec(
            num_scalar_prefetch=1,
            grid=(total // tall,),
            in_specs=whole_specs(2 + len(arrays)),
            out_specs=pl.BlockSpec((tall, wide), lambda step, place: (step, 0)),
            scratch_shapes=[parts, parts],
        ),
        compiler_params=pltpu.CompilerParams(
            vmem_limit_bytes=sum(a.size * 4 for a in arrays) + 10 * tall * wide * 4 + 8 * MIB
        ),
        cost_estimate=pl.CostEstimate(
            flops=6 * out.size * slots * depth, bytes_accessed=out.size * 4, transcendentals=0
        ),
        name="outer",
    )(place, rows_energy, cols_energy, *arrays)


def local(rows, cols, amplitudes, factors, occ_index, vir_index, occ_energy, vir_energy):
    cores = 2
    share = rows // cores
    chips = [(z, j, s) for z in range(rows) for j in range(rows) for s in range(cores)]

    def number(z, j, s):
        return z * cols + j * cores + s

    def turn(i, s):
        i = share - 1 - i
        return i if s == 0 else rows - 1 - i

    def move(x, to):
        return lax.ppermute(x, AXES, [(number(*at), number(*to(*at))) for at in chips])

    def swap(x):
        return move(x, lambda z, j, s: (z, j, 1 - s))

    def transposed(x, i):
        return move(x, lambda z, j, s: (j ^ z ^ turn(i, s), z, s))

    def reduced(x, i):
        return move(x, lambda z, j, s: (z, z ^ j ^ turn(i, s), s))

    def across(x, i):
        return move(x, lambda z, j, s: (z, j ^ turn(i, s), s))

    turns = range(share)
    row_index = lax.axis_index("row").astype(jnp.int32)
    col_index = lax.axis_index("col").astype(jnp.int32)
    core = col_index % cores
    tall, wide = amplitudes.shape

    def share_of(x):
        other = swap(x)
        return jnp.where(
            core == 0, jnp.concatenate([x, other], axis=0), jnp.concatenate([other, x], axis=0)
        )

    pieces = share_of(factors.T)
    received = [transposed(pieces, i) for i in turns]
    tied, pieces = lax.optimization_barrier((amplitudes, pieces))
    high, low = prepare(core, amplitudes, swap(tied))
    rows_energy, cols_energy = pair_energies(
        jnp.stack([row_index, col_index]), occ_index, vir_index, occ_energy, vir_energy, tall, wide
    )
    high, low, rows_energy, cols_energy = lax.optimization_barrier(
        (high, low, rows_energy, cols_energy)
    )
    arrived = [reduced(contract(received[i], high, low), i) for i in turns]
    total = functools.reduce(jnp.add, arrived)
    dressed = pieces + (total + swap(total))
    left = [across(dressed, i) for i in turns]
    left += [swap(x) for x in left]
    right = [transposed(dressed, i) for i in turns]
    right += [swap(x) for x in right]
    first = share - 1 - jnp.arange(share, dtype=jnp.int32)
    first = jnp.where(core == 0, first, rows - 1 - first)
    order = jnp.concatenate([first, rows - 1 - first])
    wanted = row_index ^ order
    at = jnp.sum(
        jnp.where(wanted[:, None] == order[None, :], jnp.arange(rows, dtype=jnp.int32)[None, :], 0), axis=1
    )
    place = jnp.concatenate([core[None], at]).astype(jnp.int32)
    left_high, left_low = left_parts(left)
    return outer(place, rows_energy, cols_energy, left_high, left_low, right)


def solution(mesh):
    rows, cols = mesh.shape["row"], mesh.shape["col"]
    return jax.shard_map(
        functools.partial(local, rows, cols),
        mesh=mesh,
        in_specs=(P("row", "col"), P("row", "col"), P(), P(), P(), P()),
        out_specs=P("row", "col"),
        check_vma=False,
    )
```

```python
import functools

import jax
import jax.numpy as jnp
from jax import lax
from jax.experimental import pallas as pl
from jax.experimental.pallas import tpu as pltpu
from jax.sharding import PartitionSpec as P

AXES = ("row", "col")
MIB = 1 << 20


def split(x):
    high = x.astype(jnp.bfloat16)
    low = (x - high.astype(jnp.float32)).astype(jnp.bfloat16)
    return high, low


def params(*arrays):
    held = sum(a.size * a.dtype.itemsize for a in arrays)
    return pltpu.CompilerParams(vmem_limit_bytes=2 * held + 4 * MIB)


def whole_specs(count):
    return [pl.BlockSpec(memory_space=pltpu.VMEM)] * count


def shape_of(shape, dtype=jnp.float32):
    return jax.ShapeDtypeStruct(shape, dtype)


def prepare_kernel(block_ref, high_ref, low_ref):
    high_ref[...], low_ref[...] = split(block_ref[...].T)


def prepare(block):
    tall, wide = block.shape
    step = min(256, tall)
    out = shape_of((wide, tall), jnp.bfloat16)
    out_spec = pl.BlockSpec((wide, step), lambda i: (0, i))
    return pl.pallas_call(
        prepare_kernel,
        out_shape=(out, out),
        grid=(tall // step,),
        in_specs=[pl.BlockSpec((step, wide), lambda i: (i, 0))],
        out_specs=[out_spec, out_spec],
        compiler_params=pltpu.CompilerParams(vmem_limit_bytes=step * wide * 32 + 4 * MIB),
        cost_estimate=pl.CostEstimate(flops=0, bytes_accessed=block.size * 8, transcendentals=0),
        name="prepare",
    )(block)


def contract_kernel(core, factors_ref, *refs):
    out_ref = refs[-1]
    rows = factors_ref.shape[0]
    parts = []
    for number, high_ref, low_ref in ((core[0], refs[0], refs[1]), (1 - core[0], refs[2], refs[3])):
        wide = high_ref.shape[0]
        high, low = split(factors_ref[:, pl.ds(pl.multiple_of(number * wide, wide), wide)])
        both = jnp.concatenate([high, low], axis=0)
        first = jnp.dot(both, high_ref[...], preferred_element_type=jnp.float32)
        second = jnp.dot(high, low_ref[...], preferred_element_type=jnp.float32)
        parts.append(first[:rows] + (first[rows:] + second))
    out_ref[...] = parts[0] + parts[1]


def contract(core, factors, own, sibling):
    wide, tall = own[0].shape
    out = shape_of((factors.shape[0], tall))
    arrays = [factors, *own, *sibling]
    return pl.pallas_call(
        contract_kernel,
        out_shape=out,
        in_specs=[pl.BlockSpec(memory_space=pltpu.SMEM)] + whole_specs(5),
        out_specs=whole_specs(1)[0],
        compiler_params=params(*arrays, out),
        cost_estimate=pl.CostEstimate(
            flops=12 * out.size * wide, bytes_accessed=own[0].size * 8, transcendentals=0
        ),
        name="contract",
    )(core.reshape(1), *arrays)


def pick(table, index):
    rows, lanes = table.shape
    length = index.shape[1]
    at_lane = lax.broadcasted_iota(jnp.int32, (lanes, length), 0) == index % lanes
    picked = jnp.dot(
        table,
        at_lane.astype(jnp.float32),
        precision=lax.Precision.HIGHEST,
        preferred_element_type=jnp.float32,
    )
    at_row = lax.broadcasted_iota(jnp.int32, (rows, length), 0) == index // lanes
    return jnp.sum(jnp.where(at_row, picked, 0.0), axis=0, keepdims=True)


def weight_kernel(place, occ_ref, vir_ref, occ_table, vir_table, out_ref):
    energies = []
    for number, length in enumerate(out_ref.shape):
        here = pl.ds(pl.multiple_of(place[number] * length, length), length)
        energies.append(pick(vir_table[...], vir_ref[:, here]) - pick(occ_table[...], occ_ref[:, here]))
    rows, cols = energies
    for start in range(0, out_ref.shape[0], 128):
        column = jnp.broadcast_to(rows[:, start : start + 128], (128, 128)).T
        wide = jnp.concatenate([column] * (out_ref.shape[1] // 128), axis=1)
        out_ref[pl.ds(start, 128), :] = -1.0 / (wide + cols)


def as_table(energies):
    lanes = 128
    padded = jnp.pad(energies, (0, -energies.shape[0] % lanes))
    return padded.reshape(-1, lanes)


def weights(place, occ_index, vir_index, occ_energy, vir_energy, rows, cols):
    occ_index, vir_index = occ_index[None, :], vir_index[None, :]
    occ_table, vir_table = as_table(occ_energy), as_table(vir_energy)
    out = shape_of((rows, cols))
    return pl.pallas_call(
        weight_kernel,
        out_shape=out,
        in_specs=[pl.BlockSpec(memory_space=pltpu.SMEM)] + whole_specs(4),
        out_specs=whole_specs(1)[0],
        compiler_params=pltpu.CompilerParams(vmem_limit_bytes=out.size * 4 + 8 * MIB),
        cost_estimate=pl.CostEstimate(flops=0, bytes_accessed=out.size * 4, transcendentals=0),
        name="weights",
    )(place, occ_index, vir_index, occ_table, vir_table)


def left_kernel(slots, *refs):
    high_ref, low_ref = refs[slots:]
    depth = refs[0].shape[0]
    step = 128 // depth
    for slot in range(0, slots, step):
        block = jnp.concatenate([refs[slot + k][...] for k in range(step)], axis=0).T
        high, low = split(block)
        here = pl.ds(slot * depth, step * depth)
        high_ref[:, here] = high
        low_ref[:, here] = low


def left_parts(left):
    slots = len(left)
    depth, total = left[0].shape
    out = shape_of((total, slots * depth), jnp.bfloat16)
    return pl.pallas_call(
        functools.partial(left_kernel, slots),
        out_shape=(out, out),
        in_specs=whole_specs(slots),
        out_specs=whole_specs(2),
        compiler_params=params(*left, out, out),
        cost_estimate=pl.CostEstimate(flops=0, bytes_accessed=out.size * 8, transcendentals=0),
        name="left_parts",
    )(*left)


CHUNKS = 4


def outer_kernel(slots, place, weights_ref, left_high, left_low, *refs):
    right = refs[:slots]
    out_ref, high_ref, low_ref, result_ref, sems = refs[slots:]
    depth = right[0].shape[0]
    total, wide = out_ref.shape
    mine = pl.ds(pl.multiple_of(place[0] * wide, wide), wide)
    for slot in range(slots):
        high, low = split(right[slot][:, mine])
        here = pl.ds(pl.multiple_of(place[1 + slot] * depth, depth), depth)
        high_ref[here, :] = high
        low_ref[here, :] = low
    tall = total // CHUNKS
    copies = []
    for chunk in range(CHUNKS):
        here = pl.ds(chunk * tall, tall)
        high, low = left_high[here, :], left_low[here, :]
        value = jnp.dot(low, high_ref[...], preferred_element_type=jnp.float32)
        value += jnp.dot(high, low_ref[...], preferred_element_type=jnp.float32)
        value += jnp.dot(high, high_ref[...], preferred_element_type=jnp.float32)
        result_ref[here, :] = value * weights_ref[here, :]
        copies.append(
            pltpu.make_async_copy(result_ref.at[here, :], out_ref.at[here, :], sems.at[chunk])
        )
        copies[-1].start()
    for copy in copies:
        copy.wait()


def outer(place, weights, left_high, left_low, right):
    slots = len(right)
    depth, total = right[0].shape
    wide = weights.shape[1]
    arrays = [weights, left_high, left_low, *right]
    out = shape_of((total, wide))
    parts = pltpu.VMEM((slots * depth, wide), jnp.bfloat16)
    return pl.pallas_call(
        functools.partial(outer_kernel, slots),
        out_shape=out,
        in_specs=[pl.BlockSpec(memory_space=pltpu.SMEM)] + whole_specs(len(arrays)),
        out_specs=pl.BlockSpec(memory_space=pl.ANY),
        scratch_shapes=[
            parts,
            parts,
            pltpu.VMEM((total, wide), jnp.float32),
            pltpu.SemaphoreType.DMA((CHUNKS,)),
        ],
        compiler_params=pltpu.CompilerParams(
            vmem_limit_bytes=sum(a.size * a.dtype.itemsize for a in arrays) + out.size * 8 + 8 * MIB
        ),
        cost_estimate=pl.CostEstimate(
            flops=6 * out.size * slots * depth, bytes_accessed=out.size * 4, transcendentals=0
        ),
        name="outer",
    )(place, *arrays)


def local(rows, cols, amplitudes, factors, occ_index, vir_index, occ_energy, vir_energy):
    cores = 2
    share = rows // cores
    chips = [(z, j, s) for z in range(rows) for j in range(rows) for s in range(cores)]

    def number(z, j, s):
        return z * cols + j * cores + s

    def turn(i, s):
        i = share - 1 - i
        return i if s == 0 else rows - 1 - i

    def move(x, to):
        return lax.ppermute(x, AXES, [(number(*at), number(*to(*at))) for at in chips])

    def swap(x):
        return move(x, lambda z, j, s: (z, j, 1 - s))

    def transposed(x, i):
        return move(x, lambda z, j, s: (j ^ z ^ turn(i, s), z, s))

    def reduced(x, i):
        return move(x, lambda z, j, s: (z, z ^ j ^ turn(i, s), s))

    def across(x, i):
        return move(x, lambda z, j, s: (z, j ^ turn(i, s), s))

    turns = range(share)
    row_index = lax.axis_index("row").astype(jnp.int32)
    col_index = lax.axis_index("col").astype(jnp.int32)
    core = col_index % cores
    tall, wide = amplitudes.shape

    def share_of(x):
        other = swap(x)
        return jnp.where(
            core == 0, jnp.concatenate([x, other], axis=0), jnp.concatenate([other, x], axis=0)
        )

    pieces = share_of(factors.T)
    received = [transposed(pieces, i) for i in turns]
    amplitudes, pieces = lax.optimization_barrier((amplitudes, pieces))
    blocks = prepare(amplitudes), prepare(swap(amplitudes))
    arrived = [reduced(contract(core, received[i], *blocks), i) for i in turns]
    total = functools.reduce(jnp.add, arrived)
    total = total + swap(total)
    total, occ_index, vir_index = lax.optimization_barrier((total, occ_index, vir_index))
    dressed = pieces + total
    factor = weights(
        jnp.stack([row_index, col_index]), occ_index, vir_index, occ_energy, vir_energy, tall, wide
    )
    right = [transposed(dressed, i) for i in turns]
    left = [across(dressed, i) for i in turns]
    right[0], left, factor = lax.optimization_barrier((right[0], left[::-1], factor))
    left = left[::-1]
    left += [swap(x) for x in left]
    right += [swap(x) for x in right]
    first = share - 1 - jnp.arange(share, dtype=jnp.int32)
    first = jnp.where(core == 0, first, rows - 1 - first)
    order = jnp.concatenate([first, rows - 1 - first])
    wanted = row_index ^ order
    at = jnp.sum(
        jnp.where(wanted[:, None] == order[None, :], jnp.arange(rows, dtype=jnp.int32)[None, :], 0), axis=1
    )
    place = jnp.concatenate([core[None], at]).astype(jnp.int32)
    left_high, left_low = left_parts(left)
    return outer(place, factor, left_high, left_low, right)


def solution(mesh):
    rows, cols = mesh.shape["row"], mesh.shape["col"]
    return jax.shard_map(
        functools.partial(local, rows, cols),
        mesh=mesh,
        in_specs=(P("row", "col"), P("row", "col"), P(), P(), P(), P()),
        out_specs=P("row", "col"),
        check_vma=False,
    )
```

```python
import functools

import jax
import jax.numpy as jnp
from jax import lax
from jax.experimental import pallas as pl
from jax.experimental.pallas import tpu as pltpu
from jax.sharding import PartitionSpec as P

AXES = ("row", "col")
MIB = 1 << 20


def split(x):
    high = x.astype(jnp.bfloat16)
    low = (x - high.astype(jnp.float32)).astype(jnp.bfloat16)
    return high, low


def params(*arrays):
    held = sum(a.size * a.dtype.itemsize for a in arrays)
    return pltpu.CompilerParams(vmem_limit_bytes=2 * held + 4 * MIB)


def whole_specs(count):
    return [pl.BlockSpec(memory_space=pltpu.VMEM)] * count


def shape_of(shape, dtype=jnp.float32):
    return jax.ShapeDtypeStruct(shape, dtype)


def prepare_kernel(block_ref, high_ref, low_ref):
    high_ref[...], low_ref[...] = split(block_ref[...].T)


def prepare(block):
    tall, wide = block.shape
    step = min(256, tall)
    out = shape_of((wide, tall), jnp.bfloat16)
    out_spec = pl.BlockSpec((wide, step), lambda i: (0, i))
    return pl.pallas_call(
        prepare_kernel,
        out_shape=(out, out),
        grid=(tall // step,),
        in_specs=[pl.BlockSpec((step, wide), lambda i: (i, 0))],
        out_specs=[out_spec, out_spec],
        compiler_params=pltpu.CompilerParams(vmem_limit_bytes=step * wide * 32 + 4 * MIB),
        cost_estimate=pl.CostEstimate(flops=0, bytes_accessed=block.size * 8, transcendentals=0),
        name="prepare",
    )(block)


def contract_kernel(slots, place, *refs):
    factors, blocks = refs[:slots], refs[slots : slots + 4]
    outs = refs[slots + 4 : 2 * slots + 4]
    both_ref = refs[-1]
    depth = factors[0].shape[0]
    rows = slots * depth
    for slot in range(slots):
        high, low = split(factors[slot][...])
        both_ref[pl.ds(pl.multiple_of(place[1 + slot] * depth, depth), depth), :] = high
        both_ref[pl.ds(pl.multiple_of(rows + place[1 + slot] * depth, depth), depth), :] = low
    total = None
    for number, high_ref, low_ref in ((place[0], *blocks[:2]), (1 - place[0], *blocks[2:])):
        wide = high_ref.shape[0]
        here = pl.ds(pl.multiple_of(number * wide, wide), wide)
        first = jnp.dot(both_ref[:, here], high_ref[...], preferred_element_type=jnp.float32)
        second = jnp.dot(both_ref[:rows, here], low_ref[...], preferred_element_type=jnp.float32)
        part = first[:rows] + (first[rows:] + second)
        total = part if total is None else total + part
    for slot in range(slots):
        outs[slot][...] = total[slot * depth : (slot + 1) * depth]


def contract(place, factors, own, sibling):
    slots = len(factors)
    depth, length = factors[0].shape
    tall = own[0].shape[1]
    out = shape_of((depth, tall))
    both = shape_of((2 * slots * depth, length), jnp.bfloat16)
    arrays = [*factors, *own, *sibling]
    return pl.pallas_call(
        functools.partial(contract_kernel, slots),
        out_shape=[out] * slots,
        in_specs=[pl.BlockSpec(memory_space=pltpu.SMEM)] + whole_specs(len(arrays)),
        out_specs=whole_specs(slots),
        scratch_shapes=[pltpu.VMEM(both.shape, both.dtype)],
        compiler_params=params(*arrays, both, *[out] * slots * 4),
        cost_estimate=pl.CostEstimate(
            flops=6 * slots * out.size * length, bytes_accessed=own[0].size * 8, transcendentals=0
        ),
        name="contract",
    )(place, *arrays)


def fetch_kernel(x_ref, out_ref):
    out_ref[...] = x_ref[...]


def fetch(x):
    return pl.pallas_call(
        fetch_kernel,
        out_shape=shape_of(x.shape),
        grid=(1,),
        in_specs=[pl.BlockSpec(x.shape, lambda i: (0, 0))],
        out_specs=pl.BlockSpec(memory_space=pltpu.VMEM),
        compiler_params=params(x, x),
        cost_estimate=pl.CostEstimate(flops=0, bytes_accessed=x.size * 8, transcendentals=0),
        name="fetch",
    )(x)


def pick(table, index):
    rows, lanes = table.shape
    length = index.shape[1]
    at_lane = lax.broadcasted_iota(jnp.int32, (lanes, length), 0) == index % lanes
    picked = jnp.dot(
        table,
        at_lane.astype(jnp.float32),
        precision=lax.Precision.HIGHEST,
        preferred_element_type=jnp.float32,
    )
    at_row = lax.broadcasted_iota(jnp.int32, (rows, length), 0) == index // lanes
    return jnp.sum(jnp.where(at_row, picked, 0.0), axis=0, keepdims=True)


def weight_kernel(place, occ_ref, vir_ref, occ_table, vir_table, out_ref):
    energies = []
    for number, length in enumerate(out_ref.shape):
        here = pl.ds(pl.multiple_of(place[number] * length, length), length)
        energies.append(pick(vir_table[...], vir_ref[:, here]) - pick(occ_table[...], occ_ref[:, here]))
    rows, cols = energies
    for start in range(0, out_ref.shape[0], 128):
        column = jnp.broadcast_to(rows[:, start : start + 128], (128, 128)).T
        wide = jnp.concatenate([column] * (out_ref.shape[1] // 128), axis=1)
        out_ref[pl.ds(start, 128), :] = -1.0 / (wide + cols)


def as_table(energies):
    lanes = 128
    padded = jnp.pad(energies, (0, -energies.shape[0] % lanes))
    return padded.reshape(-1, lanes)


def weights(place, occ_index, vir_index, occ_energy, vir_energy, rows, cols):
    occ_index, vir_index = occ_index[None, :], vir_index[None, :]
    occ_table, vir_table = as_table(occ_energy), as_table(vir_energy)
    out = shape_of((rows, cols))
    return pl.pallas_call(
        weight_kernel,
        out_shape=out,
        in_specs=[pl.BlockSpec(memory_space=pltpu.SMEM)] + whole_specs(4),
        out_specs=whole_specs(1)[0],
        compiler_params=pltpu.CompilerParams(vmem_limit_bytes=out.size * 4 + 8 * MIB),
        cost_estimate=pl.CostEstimate(flops=0, bytes_accessed=out.size * 4, transcendentals=0),
        name="weights",
    )(place, occ_index, vir_index, occ_table, vir_table)


def left_kernel(slots, *refs):
    high_ref, low_ref = refs[slots:]
    depth = refs[0].shape[0]
    step = 128 // depth
    for slot in range(0, slots, step):
        block = jnp.concatenate([refs[slot + k][...] for k in range(step)], axis=0).T
        high, low = split(block)
        here = pl.ds(slot * depth, step * depth)
        high_ref[:, here] = high
        low_ref[:, here] = low


def left_parts(left):
    slots = len(left)
    depth, total = left[0].shape
    out = shape_of((total, slots * depth), jnp.bfloat16)
    return pl.pallas_call(
        functools.partial(left_kernel, slots),
        out_shape=(out, out),
        in_specs=whole_specs(slots),
        out_specs=whole_specs(2),
        compiler_params=params(*left, out, out),
        cost_estimate=pl.CostEstimate(flops=0, bytes_accessed=out.size * 8, transcendentals=0),
        name="left_parts",
    )(*left)


CHUNKS = 2


def outer_kernel(slots, place, weights_ref, left_high, left_low, *refs):
    right = refs[:slots]
    out_ref, high_ref, low_ref, result_ref, sems = refs[slots:]
    depth = right[0].shape[0]
    total, wide = out_ref.shape
    mine = pl.ds(pl.multiple_of(place[0] * wide, wide), wide)
    for slot in range(slots):
        high, low = split(right[slot][:, mine])
        here = pl.ds(pl.multiple_of(place[1 + slot] * depth, depth), depth)
        high_ref[here, :] = high
        low_ref[here, :] = low
    step = wide // CHUNKS
    copies = []
    for chunk in range(CHUNKS):
        here = pl.ds(chunk * step, step)
        value = jnp.dot(left_low[...], high_ref[:, here], preferred_element_type=jnp.float32)
        value += jnp.dot(left_high[...], low_ref[:, here], preferred_element_type=jnp.float32)
        value += jnp.dot(left_high[...], high_ref[:, here], preferred_element_type=jnp.float32)
        result_ref[:, here] = value * weights_ref[:, here]
        copies.append(
            pltpu.make_async_copy(result_ref.at[:, here], out_ref.at[:, here], sems.at[chunk])
        )
        copies[-1].start()
    for copy in copies:
        copy.wait()


def outer(place, weights, left_high, left_low, right):
    slots = len(right)
    depth, total = right[0].shape
    wide = weights.shape[1]
    arrays = [weights, left_high, left_low, *right]
    out = shape_of((total, wide))
    parts = pltpu.VMEM((slots * depth, wide), jnp.bfloat16)
    return pl.pallas_call(
        functools.partial(outer_kernel, slots),
        out_shape=out,
        in_specs=[pl.BlockSpec(memory_space=pltpu.SMEM)] + whole_specs(len(arrays)),
        out_specs=pl.BlockSpec(memory_space=pl.ANY),
        scratch_shapes=[
            parts,
            parts,
            pltpu.VMEM((total, wide), jnp.float32),
            pltpu.SemaphoreType.DMA((CHUNKS,)),
        ],
        compiler_params=pltpu.CompilerParams(
            vmem_limit_bytes=sum(a.size * a.dtype.itemsize for a in arrays) + out.size * 8 + 8 * MIB
        ),
        cost_estimate=pl.CostEstimate(
            flops=6 * out.size * slots * depth, bytes_accessed=out.size * 4, transcendentals=0
        ),
        name="outer",
    )(place, *arrays)


def local(rows, cols, amplitudes, factors, occ_index, vir_index, occ_energy, vir_energy):
    cores = 2
    share = rows // cores
    chips = [(z, j, s) for z in range(rows) for j in range(rows) for s in range(cores)]

    def number(z, j, s):
        return z * cols + j * cores + s

    def turn(i, s):
        return i if s == 0 else rows - 1 - i

    def move(x, to):
        return lax.ppermute(x, AXES, [(number(*at), number(*to(*at))) for at in chips])

    def swap(x):
        return move(x, lambda z, j, s: (z, j, 1 - s))

    def transposed(x, i):
        return move(x, lambda z, j, s: (j ^ z ^ turn(i, s), z, s))

    def reduced(x, k):
        def to(z, j, s):
            upper = z // share ^ s
            return z, j ^ (upper * share + (share - 1 - k if upper else k)), s

        return move(x, to)

    def across(x, i):
        return move(x, lambda z, j, s: (z, j ^ turn(i, s), s))

    turns = range(share)
    row_index = lax.axis_index("row").astype(jnp.int32)
    col_index = lax.axis_index("col").astype(jnp.int32)
    core = col_index % cores
    tall, wide = amplitudes.shape

    def share_of(x, mine):
        other = swap(x)
        return jnp.where(
            core == 0, jnp.concatenate([mine, other], axis=0), jnp.concatenate([other, mine], axis=0)
        )

    first = jnp.arange(share, dtype=jnp.int32)
    mirror = share - 1 - first
    low = row_index % share ^ jnp.where(core == 0, first, mirror)
    low = jnp.where(row_index // share == core, low, share - 1 - low)
    position = jnp.concatenate([core[None], low]).astype(jnp.int32)

    pieces = share_of(factors.T, fetch(factors.T))
    received = [transposed(pieces, i) for i in turns]
    amplitudes, pieces = lax.optimization_barrier((amplitudes, pieces))
    blocks = prepare(amplitudes), prepare(swap(amplitudes))
    partial = contract(position, received, *blocks)
    arrived = [reduced(partial[k], k) for k in turns]
    total = functools.reduce(jnp.add, arrived)
    total = total + swap(total)
    total, occ_index, vir_index = lax.optimization_barrier((total, occ_index, vir_index))
    dressed = pieces + total
    factor = weights(
        jnp.stack([row_index, col_index]), occ_index, vir_index, occ_energy, vir_energy, tall, wide
    )
    right = [transposed(dressed, i) for i in turns]
    left = [across(dressed, i) for i in turns]
    right[0], left, factor = lax.optimization_barrier((right[0], left, factor))
    left += [swap(x) for x in left]
    right += [swap(x) for x in right]
    first = jnp.where(core == 0, first, rows - 1 - first)
    order = jnp.concatenate([first, rows - 1 - first])
    wanted = row_index ^ order
    at = jnp.sum(
        jnp.where(wanted[:, None] == order[None, :], jnp.arange(rows, dtype=jnp.int32)[None, :], 0), axis=1
    )
    place = jnp.concatenate([core[None], at]).astype(jnp.int32)
    left_high, left_low = left_parts(left)
    return outer(place, factor, left_high, left_low, right)


def solution(mesh):
    rows, cols = mesh.shape["row"], mesh.shape["col"]
    return jax.shard_map(
        functools.partial(local, rows, cols),
        mesh=mesh,
        in_specs=(P("row", "col"), P("row", "col"), P(), P(), P(), P()),
        out_specs=P("row", "col"),
        check_vma=False,
    )
```

```python
import functools

import jax
import jax.numpy as jnp
from jax import lax
from jax.experimental import pallas as pl
from jax.experimental.pallas import tpu as pltpu
from jax.sharding import PartitionSpec as P

AXES = ("row", "col")
MIB = 1 << 20


def split(x):
    high = x.astype(jnp.bfloat16)
    low = (x - high.astype(jnp.float32)).astype(jnp.bfloat16)
    return high, low


def params(*arrays):
    held = sum(a.size * a.dtype.itemsize for a in arrays)
    return pltpu.CompilerParams(vmem_limit_bytes=2 * held + 4 * MIB)


def whole_specs(count):
    return [pl.BlockSpec(memory_space=pltpu.VMEM)] * count


def shape_of(shape, dtype=jnp.float32):
    return jax.ShapeDtypeStruct(shape, dtype)


def prepare_kernel(block_ref, high_ref, low_ref):
    high_ref[...], low_ref[...] = split(block_ref[...].T)


def prepare(block):
    tall, wide = block.shape
    step = min(256, tall)
    out = shape_of((wide, tall), jnp.bfloat16)
    out_spec = pl.BlockSpec((wide, step), lambda i: (0, i))
    return pl.pallas_call(
        prepare_kernel,
        out_shape=(out, out),
        grid=(tall // step,),
        in_specs=[pl.BlockSpec((step, wide), lambda i: (i, 0))],
        out_specs=[out_spec, out_spec],
        compiler_params=pltpu.CompilerParams(vmem_limit_bytes=step * wide * 32 + 4 * MIB),
        cost_estimate=pl.CostEstimate(flops=0, bytes_accessed=block.size * 8, transcendentals=0),
        name="prepare",
    )(block)


def contract_kernel(core, factors_ref, *refs):
    out_ref = refs[-1]
    rows = factors_ref.shape[0]
    parts = []
    for number, high_ref, low_ref in ((core[0], refs[0], refs[1]), (1 - core[0], refs[2], refs[3])):
        wide = high_ref.shape[0]
        high, low = split(factors_ref[:, pl.ds(pl.multiple_of(number * wide, wide), wide)])
        both = jnp.concatenate([high, low], axis=0)
        first = jnp.dot(both, high_ref[...], preferred_element_type=jnp.float32)
        second = jnp.dot(high, low_ref[...], preferred_element_type=jnp.float32)
        parts.append(first[:rows] + (first[rows:] + second))
    out_ref[...] = parts[0] + parts[1]


def contract(core, factors, own, sibling):
    wide, tall = own[0].shape
    out = shape_of((factors.shape[0], tall))
    arrays = [factors, *own, *sibling]
    return pl.pallas_call(
        contract_kernel,
        out_shape=out,
        in_specs=[pl.BlockSpec(memory_space=pltpu.SMEM)] + whole_specs(5),
        out_specs=whole_specs(1)[0],
        compiler_params=params(*arrays, out),
        cost_estimate=pl.CostEstimate(
            flops=12 * out.size * wide, bytes_accessed=own[0].size * 8, transcendentals=0
        ),
        name="contract",
    )(core.reshape(1), *arrays)


def fetch_kernel(x_ref, out_ref):
    out_ref[...] = x_ref[...]


def fetch(x):
    return pl.pallas_call(
        fetch_kernel,
        out_shape=shape_of(x.shape),
        grid=(1,),
        in_specs=[pl.BlockSpec(x.shape, lambda i: (0, 0))],
        out_specs=pl.BlockSpec(memory_space=pltpu.VMEM),
        compiler_params=params(x, x),
        cost_estimate=pl.CostEstimate(flops=0, bytes_accessed=x.size * 8, transcendentals=0),
        name="fetch",
    )(x)


def pick(table, index):
    rows, lanes = table.shape
    length = index.shape[1]
    at_lane = lax.broadcasted_iota(jnp.int32, (lanes, length), 0) == index % lanes
    picked = jnp.dot(
        table,
        at_lane.astype(jnp.float32),
        precision=lax.Precision.HIGHEST,
        preferred_element_type=jnp.float32,
    )
    at_row = lax.broadcasted_iota(jnp.int32, (rows, length), 0) == index // lanes
    return jnp.sum(jnp.where(at_row, picked, 0.0), axis=0, keepdims=True)


def weight_kernel(place, occ_ref, vir_ref, occ_table, vir_table, out_ref):
    energies = []
    for number, length in enumerate(out_ref.shape):
        here = pl.ds(pl.multiple_of(place[number] * length, length), length)
        energies.append(pick(vir_table[...], vir_ref[:, here]) - pick(occ_table[...], occ_ref[:, here]))
    rows, cols = energies
    for start in range(0, out_ref.shape[0], 128):
        column = jnp.broadcast_to(rows[:, start : start + 128], (128, 128)).T
        wide = jnp.concatenate([column] * (out_ref.shape[1] // 128), axis=1)
        out_ref[pl.ds(start, 128), :] = -1.0 / (wide + cols)


def as_table(energies):
    lanes = 128
    padded = jnp.pad(energies, (0, -energies.shape[0] % lanes))
    return padded.reshape(-1, lanes)


def weights(place, occ_index, vir_index, occ_energy, vir_energy, rows, cols):
    occ_index, vir_index = occ_index[None, :], vir_index[None, :]
    occ_table, vir_table = as_table(occ_energy), as_table(vir_energy)
    out = shape_of((rows, cols))
    return pl.pallas_call(
        weight_kernel,
        out_shape=out,
        in_specs=[pl.BlockSpec(memory_space=pltpu.SMEM)] + whole_specs(4),
        out_specs=whole_specs(1)[0],
        compiler_params=pltpu.CompilerParams(vmem_limit_bytes=out.size * 4 + 8 * MIB),
        cost_estimate=pl.CostEstimate(flops=0, bytes_accessed=out.size * 4, transcendentals=0),
        name="weights",
    )(place, occ_index, vir_index, occ_table, vir_table)


def left_kernel(slots, *refs):
    high_ref, low_ref = refs[slots:]
    depth = refs[0].shape[0]
    step = 128 // depth
    for slot in range(0, slots, step):
        block = jnp.concatenate([refs[slot + k][...] for k in range(step)], axis=0).T
        high, low = split(block)
        here = pl.ds(slot * depth, step * depth)
        high_ref[:, here] = high
        low_ref[:, here] = low


def left_parts(left):
    slots = len(left)
    depth, total = left[0].shape
    out = shape_of((total, slots * depth), jnp.bfloat16)
    return pl.pallas_call(
        functools.partial(left_kernel, slots),
        out_shape=(out, out),
        in_specs=whole_specs(slots),
        out_specs=whole_specs(2),
        compiler_params=params(*left, out, out),
        cost_estimate=pl.CostEstimate(flops=0, bytes_accessed=out.size * 8, transcendentals=0),
        name="left_parts",
    )(*left)


def outer_kernel(slots, place, weights_ref, left_high, left_low, *refs):
    right = refs[:slots]
    out_ref, high_ref, low_ref = refs[slots:]
    depth = right[0].shape[0]
    tall, wide = out_ref.shape
    step = pl.program_id(0)

    @pl.when(step == 0)
    def _():
        mine = pl.ds(pl.multiple_of(place[0] * wide, wide), wide)
        for slot in range(slots):
            high, low = split(right[slot][:, mine])
            here = pl.ds(pl.multiple_of(place[1 + slot] * depth, depth), depth)
            high_ref[here, :] = high
            low_ref[here, :] = low

    here = pl.ds(pl.multiple_of(step * tall, tall), tall)
    high, low = left_high[here, :], left_low[here, :]
    value = jnp.dot(low, high_ref[...], preferred_element_type=jnp.float32)
    value += jnp.dot(high, low_ref[...], preferred_element_type=jnp.float32)
    value += jnp.dot(high, high_ref[...], preferred_element_type=jnp.float32)
    out_ref[...] = value * weights_ref[here, :]


def outer(place, weights, left_high, left_low, right):
    slots = len(right)
    depth, total = right[0].shape
    wide = weights.shape[1]
    tall = min(1024, total)
    arrays = [weights, left_high, left_low, *right]
    out = shape_of((total, wide))
    parts = pltpu.VMEM((slots * depth, wide), jnp.bfloat16)
    return pl.pallas_call(
        functools.partial(outer_kernel, slots),
        out_shape=out,
        grid_spec=pltpu.PrefetchScalarGridSpec(
            num_scalar_prefetch=1,
            grid=(total // tall,),
            in_specs=whole_specs(len(arrays)),
            out_specs=pl.BlockSpec((tall, wide), lambda step, place: (step, 0)),
            scratch_shapes=[parts, parts],
        ),
        compiler_params=pltpu.CompilerParams(
            vmem_limit_bytes=sum(a.size * a.dtype.itemsize for a in arrays) + 20 * tall * wide + 4 * MIB
        ),
        cost_estimate=pl.CostEstimate(
            flops=6 * out.size * slots * depth, bytes_accessed=out.size * 4, transcendentals=0
        ),
        name="outer",
    )(place, *arrays)


def local(rows, cols, amplitudes, factors, occ_index, vir_index, occ_energy, vir_energy):
    cores = 2
    share = rows // cores
    chips = [(z, j, s) for z in range(rows) for j in range(rows) for s in range(cores)]

    def number(z, j, s):
        return z * cols + j * cores + s

    def turn(i, s):
        return i if s == 0 else rows - 1 - i

    def move(x, to):
        return lax.ppermute(x, AXES, [(number(*at), number(*to(*at))) for at in chips])

    def swap(x):
        return move(x, lambda z, j, s: (z, j, 1 - s))

    def transposed(x, i):
        return move(x, lambda z, j, s: (j ^ z ^ turn(i, s), z, s))

    def reduced(x, i):
        return move(x, lambda z, j, s: (z, z ^ j ^ turn(i, s), s))

    def across(x, i):
        return move(x, lambda z, j, s: (z, j ^ turn(i, s), s))

    turns = range(share)
    row_index = lax.axis_index("row").astype(jnp.int32)
    col_index = lax.axis_index("col").astype(jnp.int32)
    core = col_index % cores
    tall, wide = amplitudes.shape

    def share_of(x, mine):
        other = swap(x)
        return jnp.where(
            core == 0, jnp.concatenate([mine, other], axis=0), jnp.concatenate([other, mine], axis=0)
        )

    first = jnp.arange(share, dtype=jnp.int32)
    pieces = share_of(factors.T, fetch(factors.T))
    received = [transposed(pieces, i) for i in turns]
    amplitudes, pieces = lax.optimization_barrier((amplitudes, pieces))
    blocks = prepare(amplitudes), prepare(swap(amplitudes))
    partial = [contract(core, x, *blocks) for x in received]
    arrived = [reduced(partial[i], i) for i in turns]
    total = functools.reduce(jnp.add, arrived)
    total = total + swap(total)
    total, occ_index, vir_index = lax.optimization_barrier((total, occ_index, vir_index))
    dressed = pieces + total
    factor = weights(
        jnp.stack([row_index, col_index]), occ_index, vir_index, occ_energy, vir_energy, tall, wide
    )
    right = [transposed(dressed, i) for i in turns]
    left = [across(dressed, i) for i in turns]
    left[1], right[0], factor = lax.optimization_barrier((left[1], right[0], factor))
    right[0], left[0] = lax.optimization_barrier((right[0], left[0]))
    left += [swap(x) for x in left]
    right += [swap(x) for x in right]
    first = jnp.where(core == 0, first, rows - 1 - first)
    order = jnp.concatenate([first, rows - 1 - first])
    wanted = row_index ^ order
    at = jnp.sum(
        jnp.where(wanted[:, None] == order[None, :], jnp.arange(rows, dtype=jnp.int32)[None, :], 0), axis=1
    )
    place = jnp.concatenate([core[None], at]).astype(jnp.int32)
    left_high, left_low = left_parts(left)
    return outer(place, factor, left_high, left_low, right)


def solution(mesh):
    rows, cols = mesh.shape["row"], mesh.shape["col"]
    return jax.shard_map(
        functools.partial(local, rows, cols),
        mesh=mesh,
        in_specs=(P("row", "col"), P("row", "col"), P(), P(), P(), P()),
        out_specs=P("row", "col"),
        check_vma=False,
    )
```

```python
import functools

import jax
import jax.numpy as jnp
from jax import lax
from jax.experimental import pallas as pl
from jax.experimental.pallas import tpu as pltpu
from jax.sharding import PartitionSpec as P

AXES = ("row", "col")
MIB = 1 << 20


def split(x):
    high = x.astype(jnp.bfloat16)
    low = (x - high.astype(jnp.float32)).astype(jnp.bfloat16)
    return high, low


def params(*arrays):
    held = sum(a.size * a.dtype.itemsize for a in arrays)
    return pltpu.CompilerParams(vmem_limit_bytes=2 * held + 4 * MIB)


def whole_specs(count):
    return [pl.BlockSpec(memory_space=pltpu.VMEM)] * count


def shape_of(shape, dtype=jnp.float32):
    return jax.ShapeDtypeStruct(shape, dtype)


def prepare_kernel(block_ref, high_ref, low_ref):
    high_ref[...], low_ref[...] = split(block_ref[...].T)


def prepare(block):
    tall, wide = block.shape
    step = min(256, tall)
    out = shape_of((wide, tall), jnp.bfloat16)
    out_spec = pl.BlockSpec((wide, step), lambda i: (0, i))
    return pl.pallas_call(
        prepare_kernel,
        out_shape=(out, out),
        grid=(tall // step,),
        in_specs=[pl.BlockSpec((step, wide), lambda i: (i, 0))],
        out_specs=[out_spec, out_spec],
        compiler_params=pltpu.CompilerParams(vmem_limit_bytes=step * wide * 32 + 4 * MIB),
        cost_estimate=pl.CostEstimate(flops=0, bytes_accessed=block.size * 8, transcendentals=0),
        name="prepare",
    )(block)


def contract_kernel(core, factors_ref, *refs):
    out_ref = refs[-1]
    rows = factors_ref.shape[0]
    parts = []
    for number, high_ref, low_ref in ((core[0], refs[0], refs[1]), (1 - core[0], refs[2], refs[3])):
        wide = high_ref.shape[0]
        high, low = split(factors_ref[:, pl.ds(pl.multiple_of(number * wide, wide), wide)])
        both = jnp.concatenate([high, low], axis=0)
        first = jnp.dot(both, high_ref[...], preferred_element_type=jnp.float32)
        second = jnp.dot(high, low_ref[...], preferred_element_type=jnp.float32)
        parts.append(first[:rows] + (first[rows:] + second))
    out_ref[...] = parts[0] + parts[1]


def contract(core, factors, own, sibling):
    wide, tall = own[0].shape
    out = shape_of((factors.shape[0], tall))
    arrays = [factors, *own, *sibling]
    return pl.pallas_call(
        contract_kernel,
        out_shape=out,
        in_specs=[pl.BlockSpec(memory_space=pltpu.SMEM)] + whole_specs(5),
        out_specs=whole_specs(1)[0],
        compiler_params=params(*arrays, out),
        cost_estimate=pl.CostEstimate(
            flops=12 * out.size * wide, bytes_accessed=own[0].size * 8, transcendentals=0
        ),
        name="contract",
    )(core.reshape(1), *arrays)


def fetch_kernel(x_ref, out_ref):
    out_ref[...] = x_ref[...]


def fetch(x):
    return pl.pallas_call(
        fetch_kernel,
        out_shape=shape_of(x.shape),
        grid=(1,),
        in_specs=[pl.BlockSpec(x.shape, lambda i: (0, 0))],
        out_specs=pl.BlockSpec(memory_space=pltpu.VMEM),
        compiler_params=params(x, x),
        cost_estimate=pl.CostEstimate(flops=0, bytes_accessed=x.size * 8, transcendentals=0),
        name="fetch",
    )(x)


def pick(table, index):
    rows, lanes = table.shape
    length = index.shape[1]
    at_lane = lax.broadcasted_iota(jnp.int32, (lanes, length), 0) == index % lanes
    picked = jnp.dot(
        table,
        at_lane.astype(jnp.float32),
        precision=lax.Precision.HIGHEST,
        preferred_element_type=jnp.float32,
    )
    at_row = lax.broadcasted_iota(jnp.int32, (rows, length), 0) == index // lanes
    return jnp.sum(jnp.where(at_row, picked, 0.0), axis=0, keepdims=True)


def weight_kernel(place, occ_ref, vir_ref, occ_table, vir_table, out_ref):
    energies = []
    for number, length in enumerate(out_ref.shape):
        here = pl.ds(pl.multiple_of(place[number] * length, length), length)
        energies.append(pick(vir_table[...], vir_ref[:, here]) - pick(occ_table[...], occ_ref[:, here]))
    rows, cols = energies
    for start in range(0, out_ref.shape[0], 128):
        column = jnp.broadcast_to(rows[:, start : start + 128], (128, 128)).T
        wide = jnp.concatenate([column] * (out_ref.shape[1] // 128), axis=1)
        out_ref[pl.ds(start, 128), :] = -1.0 / (wide + cols)


def as_table(energies):
    lanes = 128
    padded = jnp.pad(energies, (0, -energies.shape[0] % lanes))
    return padded.reshape(-1, lanes)


def weights(place, occ_index, vir_index, occ_energy, vir_energy, rows, cols):
    occ_index, vir_index = occ_index[None, :], vir_index[None, :]
    occ_table, vir_table = as_table(occ_energy), as_table(vir_energy)
    out = shape_of((rows, cols))
    return pl.pallas_call(
        weight_kernel,
        out_shape=out,
        in_specs=[pl.BlockSpec(memory_space=pltpu.SMEM)] + whole_specs(4),
        out_specs=whole_specs(1)[0],
        compiler_params=pltpu.CompilerParams(vmem_limit_bytes=out.size * 4 + 8 * MIB),
        cost_estimate=pl.CostEstimate(flops=0, bytes_accessed=out.size * 4, transcendentals=0),
        name="weights",
    )(place, occ_index, vir_index, occ_table, vir_table)


def left_kernel(slots, *refs):
    high_ref, low_ref = refs[slots:]
    depth = refs[0].shape[0]
    step = 128 // depth
    for slot in range(0, slots, step):
        block = jnp.concatenate([refs[slot + k][...] for k in range(step)], axis=0).T
        high, low = split(block)
        here = pl.ds(slot * depth, step * depth)
        high_ref[:, here] = high
        low_ref[:, here] = low


def left_parts(left):
    slots = len(left)
    depth, total = left[0].shape
    out = shape_of((total, slots * depth), jnp.bfloat16)
    return pl.pallas_call(
        functools.partial(left_kernel, slots),
        out_shape=(out, out),
        in_specs=whole_specs(slots),
        out_specs=whole_specs(2),
        compiler_params=params(*left, out, out),
        cost_estimate=pl.CostEstimate(flops=0, bytes_accessed=out.size * 8, transcendentals=0),
        name="left_parts",
    )(*left)


CHUNKS = 4


def outer_kernel(slots, place, weights_ref, left_high, left_low, *refs):
    right = refs[:slots]
    out_ref, high_ref, low_ref, result_ref, sems = refs[slots:]
    depth = right[0].shape[0]
    total, wide = out_ref.shape
    mine = pl.ds(pl.multiple_of(place[0] * wide, wide), wide)
    for slot in range(slots):
        high, low = split(right[slot][:, mine])
        here = pl.ds(pl.multiple_of(place[1 + slot] * depth, depth), depth)
        high_ref[here, :] = high
        low_ref[here, :] = low
    tall = total // CHUNKS
    copies = []
    for chunk in range(CHUNKS):
        here = pl.ds(chunk * tall, tall)
        high, low = left_high[here, :], left_low[here, :]
        value = jnp.dot(low, high_ref[...], preferred_element_type=jnp.float32)
        value += jnp.dot(high, low_ref[...], preferred_element_type=jnp.float32)
        value += jnp.dot(high, high_ref[...], preferred_element_type=jnp.float32)
        result_ref[here, :] = value * weights_ref[here, :]
        copies.append(
            pltpu.make_async_copy(result_ref.at[here, :], out_ref.at[here, :], sems.at[chunk])
        )
        copies[-1].start()
    for copy in copies:
        copy.wait()


def outer(place, weights, left_high, left_low, right):
    slots = len(right)
    depth, total = right[0].shape
    wide = weights.shape[1]
    arrays = [weights, left_high, left_low, *right]
    out = shape_of((total, wide))
    parts = pltpu.VMEM((slots * depth, wide), jnp.bfloat16)
    return pl.pallas_call(
        functools.partial(outer_kernel, slots),
        out_shape=out,
        in_specs=[pl.BlockSpec(memory_space=pltpu.SMEM)] + whole_specs(len(arrays)),
        out_specs=pl.BlockSpec(memory_space=pl.ANY),
        scratch_shapes=[
            parts,
            parts,
            pltpu.VMEM((total, wide), jnp.float32),
            pltpu.SemaphoreType.DMA((CHUNKS,)),
        ],
        compiler_params=pltpu.CompilerParams(
            vmem_limit_bytes=sum(a.size * a.dtype.itemsize for a in arrays) + out.size * 8 + 8 * MIB
        ),
        cost_estimate=pl.CostEstimate(
            flops=6 * out.size * slots * depth, bytes_accessed=out.size * 4, transcendentals=0
        ),
        name="outer",
    )(place, *arrays)


def local(rows, cols, amplitudes, factors, occ_index, vir_index, occ_energy, vir_energy):
    cores = 2
    share = rows // cores
    chips = [(z, j, s) for z in range(rows) for j in range(rows) for s in range(cores)]

    def number(z, j, s):
        return z * cols + j * cores + s

    def turn(i, s):
        return i if s == 0 else rows - 1 - i

    def move(x, to):
        return lax.ppermute(x, AXES, [(number(*at), number(*to(*at))) for at in chips])

    def swap(x):
        return move(x, lambda z, j, s: (z, j, 1 - s))

    def turned(z, s, i):
        low = z % share ^ i
        return rows - 1 - low if s else low

    def transposed(x, i):
        def to(z, j, s):
            side, low = divmod(j ^ z, share)
            low = share - 1 - low if side else low
            return (s ^ z // share) * share + (low ^ i), z, side

        return move(x, to)

    def reduced(x, i):
        return move(x, lambda z, j, s: (z, j ^ turned(z, s, i), s))

    def across(x, i):
        return move(x, lambda z, j, s: (z, j ^ turn(i, s), s))

    def within_half(x, v):
        return move(x, lambda z, j, s: (z ^ v, j, s))

    turns = range(share)
    row_index = lax.axis_index("row").astype(jnp.int32)
    col_index = lax.axis_index("col").astype(jnp.int32)
    core = col_index % cores
    tall, wide = amplitudes.shape

    def share_of(x, mine):
        other = swap(x)
        return jnp.where(
            core == 0, jnp.concatenate([mine, other], axis=0), jnp.concatenate([other, mine], axis=0)
        )

    first = jnp.arange(share, dtype=jnp.int32)
    pieces = share_of(factors.T, fetch(factors.T))
    received = [transposed(pieces, i) for i in turns]
    amplitudes, pieces = lax.optimization_barrier((amplitudes, pieces))
    blocks = prepare(amplitudes), prepare(swap(amplitudes))
    partial = [contract(core, x, *blocks) for x in received]
    arrived = [reduced(partial[i], i) for i in turns]
    total = functools.reduce(jnp.add, arrived)
    total = total + swap(total)
    total, occ_index, vir_index = lax.optimization_barrier((total, occ_index, vir_index))
    dressed = pieces + total
    factor = weights(
        jnp.stack([row_index, col_index]), occ_index, vir_index, occ_energy, vir_energy, tall, wide
    )
    left = [across(dressed, i) for i in turns]
    right = [transposed(dressed, 0)]
    right += [within_half(right[0], v) for v in range(1, share)]
    left, factor = lax.optimization_barrier((left[::-1], factor))
    left = left[::-1]
    left += [swap(x) for x in left]
    right += [swap(x) for x in right]
    order = jnp.where(core == 0, first, rows - 1 - first)
    order = jnp.concatenate([order, rows - 1 - order])
    low = row_index % share ^ first
    lower, upper = low, rows - 1 - low
    wanted = jnp.concatenate(
        [jnp.where(core == 0, lower, upper), jnp.where(core == 0, upper, lower)]
    )
    at = jnp.sum(
        jnp.where(wanted[:, None] == order[None, :], jnp.arange(rows, dtype=jnp.int32)[None, :], 0), axis=1
    )
    place = jnp.concatenate([core[None], at]).astype(jnp.int32)
    left_high, left_low = left_parts(left)
    return outer(place, factor, left_high, left_low, right)


def solution(mesh):
    rows, cols = mesh.shape["row"], mesh.shape["col"]
    return jax.shard_map(
        functools.partial(local, rows, cols),
        mesh=mesh,
        in_specs=(P("row", "col"), P("row", "col"), P(), P(), P(), P()),
        out_specs=P("row", "col"),
        check_vma=False,
    )
```

```python
import functools

import jax
import jax.numpy as jnp
from jax import lax
from jax.experimental import pallas as pl
from jax.experimental.pallas import tpu as pltpu
from jax.sharding import PartitionSpec as P

AXES = ("row", "col")
MIB = 1 << 20


def split(x):
    high = x.astype(jnp.bfloat16)
    low = (x - high.astype(jnp.float32)).astype(jnp.bfloat16)
    return high, low


def params(*arrays):
    held = sum(a.size * a.dtype.itemsize for a in arrays)
    return pltpu.CompilerParams(vmem_limit_bytes=2 * held + 4 * MIB)


def whole_specs(count):
    return [pl.BlockSpec(memory_space=pltpu.VMEM)] * count


def shape_of(shape, dtype=jnp.float32):
    return jax.ShapeDtypeStruct(shape, dtype)


def prepare_kernel(block_ref, high_ref, low_ref):
    high_ref[...], low_ref[...] = split(block_ref[...].T)


def prepare(block):
    tall, wide = block.shape
    step = min(256, tall)
    out = shape_of((wide, tall), jnp.bfloat16)
    out_spec = pl.BlockSpec((wide, step), lambda i: (0, i))
    return pl.pallas_call(
        prepare_kernel,
        out_shape=(out, out),
        grid=(tall // step,),
        in_specs=[pl.BlockSpec((step, wide), lambda i: (i, 0))],
        out_specs=[out_spec, out_spec],
        compiler_params=pltpu.CompilerParams(vmem_limit_bytes=step * wide * 32 + 4 * MIB),
        cost_estimate=pl.CostEstimate(flops=0, bytes_accessed=block.size * 8, transcendentals=0),
        name="prepare",
    )(block)


def contract_kernel(core, factors_ref, *refs):
    out_ref = refs[-1]
    rows = factors_ref.shape[0]
    parts = []
    for number, high_ref, low_ref in ((core[0], refs[0], refs[1]), (1 - core[0], refs[2], refs[3])):
        wide = high_ref.shape[0]
        high, low = split(factors_ref[:, pl.ds(pl.multiple_of(number * wide, wide), wide)])
        both = jnp.concatenate([high, low], axis=0)
        first = jnp.dot(both, high_ref[...], preferred_element_type=jnp.float32)
        second = jnp.dot(high, low_ref[...], preferred_element_type=jnp.float32)
        parts.append(first[:rows] + (first[rows:] + second))
    out_ref[...] = parts[0] + parts[1]


def contract(core, factors, own, sibling):
    wide, tall = own[0].shape
    out = shape_of((factors.shape[0], tall))
    arrays = [factors, *own, *sibling]
    return pl.pallas_call(
        contract_kernel,
        out_shape=out,
        in_specs=[pl.BlockSpec(memory_space=pltpu.SMEM)] + whole_specs(5),
        out_specs=whole_specs(1)[0],
        compiler_params=params(*arrays, out),
        cost_estimate=pl.CostEstimate(
            flops=12 * out.size * wide, bytes_accessed=own[0].size * 8, transcendentals=0
        ),
        name="contract",
    )(core.reshape(1), *arrays)


def fetch_kernel(x_ref, out_ref):
    out_ref[...] = x_ref[...]


def fetch(x):
    return pl.pallas_call(
        fetch_kernel,
        out_shape=shape_of(x.shape),
        grid=(1,),
        in_specs=[pl.BlockSpec(x.shape, lambda i: (0, 0))],
        out_specs=pl.BlockSpec(memory_space=pltpu.VMEM),
        compiler_params=params(x, x),
        cost_estimate=pl.CostEstimate(flops=0, bytes_accessed=x.size * 8, transcendentals=0),
        name="fetch",
    )(x)


def pick(table, index):
    rows, lanes = table.shape
    length = index.shape[1]
    at_lane = lax.broadcasted_iota(jnp.int32, (lanes, length), 0) == index % lanes
    picked = jnp.dot(
        table,
        at_lane.astype(jnp.float32),
        precision=lax.Precision.HIGHEST,
        preferred_element_type=jnp.float32,
    )
    at_row = lax.broadcasted_iota(jnp.int32, (rows, length), 0) == index // lanes
    return jnp.sum(jnp.where(at_row, picked, 0.0), axis=0, keepdims=True)


def weight_kernel(place, occ_ref, vir_ref, occ_table, vir_table, out_ref):
    energies = []
    for number, length in enumerate(out_ref.shape):
        here = pl.ds(pl.multiple_of(place[number] * length, length), length)
        energies.append(pick(vir_table[...], vir_ref[:, here]) - pick(occ_table[...], occ_ref[:, here]))
    rows, cols = energies
    for start in range(0, out_ref.shape[0], 128):
        column = jnp.broadcast_to(rows[:, start : start + 128], (128, 128)).T
        wide = jnp.concatenate([column] * (out_ref.shape[1] // 128), axis=1)
        out_ref[pl.ds(start, 128), :] = -1.0 / (wide + cols)


def as_table(energies):
    lanes = 128
    padded = jnp.pad(energies, (0, -energies.shape[0] % lanes))
    return padded.reshape(-1, lanes)


def weights(place, occ_index, vir_index, occ_energy, vir_energy, rows, cols):
    occ_index, vir_index = occ_index[None, :], vir_index[None, :]
    occ_table, vir_table = as_table(occ_energy), as_table(vir_energy)
    out = shape_of((rows, cols))
    return pl.pallas_call(
        weight_kernel,
        out_shape=out,
        in_specs=[pl.BlockSpec(memory_space=pltpu.SMEM)] + whole_specs(4),
        out_specs=whole_specs(1)[0],
        compiler_params=pltpu.CompilerParams(vmem_limit_bytes=out.size * 4 + 8 * MIB),
        cost_estimate=pl.CostEstimate(flops=0, bytes_accessed=out.size * 4, transcendentals=0),
        name="weights",
    )(place, occ_index, vir_index, occ_table, vir_table)


def left_kernel(slots, *refs):
    high_ref, low_ref = refs[slots:]
    depth = refs[0].shape[0]
    step = 128 // depth
    for slot in range(0, slots, step):
        block = jnp.concatenate([refs[slot + k][...] for k in range(step)], axis=0).T
        high, low = split(block)
        here = pl.ds(slot * depth, step * depth)
        high_ref[:, here] = high
        low_ref[:, here] = low


def left_parts(left):
    slots = len(left)
    depth, total = left[0].shape
    out = shape_of((total, slots * depth), jnp.bfloat16)
    return pl.pallas_call(
        functools.partial(left_kernel, slots),
        out_shape=(out, out),
        in_specs=whole_specs(slots),
        out_specs=whole_specs(2),
        compiler_params=params(*left, out, out),
        cost_estimate=pl.CostEstimate(flops=0, bytes_accessed=out.size * 8, transcendentals=0),
        name="left_parts",
    )(*left)


CHUNKS = 4


def outer_kernel(spots, depth, place, weights_ref, left_high, left_low, *refs):
    right = refs[: len(spots)]
    out_ref, high_ref, low_ref, result_ref, sems = refs[len(spots) :]
    total, wide = out_ref.shape
    mine = pl.ds(pl.multiple_of(place[0] * wide, wide), wide)
    for ref, (slot, offset) in zip(right, spots):
        high, low = split(ref[:, mine])
        here = pl.ds(pl.multiple_of(place[1 + slot] * depth + offset, ref.shape[0]), ref.shape[0])
        high_ref[here, :] = high
        low_ref[here, :] = low
    tall = total // CHUNKS
    copies = []
    for chunk in range(CHUNKS):
        here = pl.ds(chunk * tall, tall)
        high, low = left_high[here, :], left_low[here, :]
        value = jnp.dot(low, high_ref[...], preferred_element_type=jnp.float32)
        value += jnp.dot(high, low_ref[...], preferred_element_type=jnp.float32)
        value += jnp.dot(high, high_ref[...], preferred_element_type=jnp.float32)
        result_ref[here, :] = value * weights_ref[here, :]
        copies.append(
            pltpu.make_async_copy(result_ref.at[here, :], out_ref.at[here, :], sems.at[chunk])
        )
        copies[-1].start()
    for copy in copies:
        copy.wait()


def outer(place, weights, left_high, left_low, right, spots):
    total, inner = left_high.shape
    depth = right[0].shape[0]
    wide = weights.shape[1]
    arrays = [weights, left_high, left_low, *right]
    out = shape_of((total, wide))
    parts = pltpu.VMEM((inner, wide), jnp.bfloat16)
    return pl.pallas_call(
        functools.partial(outer_kernel, spots, depth),
        out_shape=out,
        in_specs=[pl.BlockSpec(memory_space=pltpu.SMEM)] + whole_specs(len(arrays)),
        out_specs=pl.BlockSpec(memory_space=pl.ANY),
        scratch_shapes=[
            parts,
            parts,
            pltpu.VMEM((total, wide), jnp.float32),
            pltpu.SemaphoreType.DMA((CHUNKS,)),
        ],
        compiler_params=pltpu.CompilerParams(
            vmem_limit_bytes=sum(a.size * a.dtype.itemsize for a in arrays) + out.size * 8 + 8 * MIB
        ),
        cost_estimate=pl.CostEstimate(
            flops=6 * out.size * inner, bytes_accessed=out.size * 4, transcendentals=0
        ),
        name="outer",
    )(place, *arrays)


def local(rows, cols, amplitudes, factors, occ_index, vir_index, occ_energy, vir_energy):
    cores = 2
    share = rows // cores
    chips = [(z, j, s) for z in range(rows) for j in range(rows) for s in range(cores)]

    def number(z, j, s):
        return z * cols + j * cores + s

    def turn(i, s):
        return i if s == 0 else rows - 1 - i

    def move(x, to):
        return lax.ppermute(x, AXES, [(number(*at), number(*to(*at))) for at in chips])

    def swap(x):
        return move(x, lambda z, j, s: (z, j, 1 - s))

    def turned(z, s, i):
        low = z % share ^ i
        return rows - 1 - low if s else low

    def transposed(x, i):
        def to(z, j, s):
            side, low = divmod(j ^ z, share)
            low = share - 1 - low if side else low
            return (s ^ z // share) * share + (low ^ i), z, side

        return move(x, to)

    def reduced(x, i):
        return move(x, lambda z, j, s: (z, j ^ turned(z, s, i), s))

    def across(x, i):
        return move(x, lambda z, j, s: (z, j ^ turn(i, s), s))

    def within_half(x, v):
        return move(x, lambda z, j, s: (z ^ v, j, s))

    turns = range(share)
    row_index = lax.axis_index("row").astype(jnp.int32)
    col_index = lax.axis_index("col").astype(jnp.int32)
    core = col_index % cores
    tall, wide = amplitudes.shape

    def share_of(x, mine):
        other = swap(x)
        return jnp.where(
            core == 0, jnp.concatenate([mine, other], axis=0), jnp.concatenate([other, mine], axis=0)
        )

    first = jnp.arange(share, dtype=jnp.int32)
    pieces = share_of(factors.T, fetch(factors.T))
    received = [transposed(pieces, i) for i in turns]
    amplitudes, pieces = lax.optimization_barrier((amplitudes, pieces))
    blocks = prepare(amplitudes), prepare(swap(amplitudes))
    partial = [contract(core, x, *blocks) for x in received]
    arrived = [reduced(partial[i], i) for i in turns]
    total = functools.reduce(jnp.add, arrived)
    total = total + swap(total)
    total, occ_index, vir_index = lax.optimization_barrier((total, occ_index, vir_index))
    dressed = pieces + total
    factor = weights(
        jnp.stack([row_index, col_index]), occ_index, vir_index, occ_energy, vir_energy, tall, wide
    )
    left = [across(dressed, i) for i in turns]
    part = dressed.shape[0] // 2
    right, spots = [transposed(dressed, 0)], [(0, 0)]
    for v in range(1, share):
        right += [transposed(dressed[part:], v), within_half(right[0][:part], v)]
        spots += [(v, part), (v, 0)]
    spots += [(share + slot, offset) for slot, offset in spots]
    left[1], factor = lax.optimization_barrier((left[1], factor))
    left += [swap(x) for x in left]
    right += [swap(x) for x in right]
    order = jnp.where(core == 0, first, rows - 1 - first)
    order = jnp.concatenate([order, rows - 1 - order])
    low = row_index % share ^ first
    lower, upper = low, rows - 1 - low
    wanted = jnp.concatenate(
        [jnp.where(core == 0, lower, upper), jnp.where(core == 0, upper, lower)]
    )
    at = jnp.sum(
        jnp.where(wanted[:, None] == order[None, :], jnp.arange(rows, dtype=jnp.int32)[None, :], 0), axis=1
    )
    place = jnp.concatenate([core[None], at]).astype(jnp.int32)
    left_high, left_low = left_parts(left)
    return outer(place, factor, left_high, left_low, right, spots)


def solution(mesh):
    rows, cols = mesh.shape["row"], mesh.shape["col"]
    return jax.shard_map(
        functools.partial(local, rows, cols),
        mesh=mesh,
        in_specs=(P("row", "col"), P("row", "col"), P(), P(), P(), P()),
        out_specs=P("row", "col"),
        check_vma=False,
    )
```

```python
import functools

import jax
import jax.numpy as jnp
from jax import lax
from jax.experimental import pallas as pl
from jax.experimental.pallas import tpu as pltpu
from jax.sharding import PartitionSpec as P

AXES = ("row", "col")
MIB = 1 << 20


def split(x):
    high = x.astype(jnp.bfloat16)
    low = (x - high.astype(jnp.float32)).astype(jnp.bfloat16)
    return high, low


def params(*arrays):
    held = sum(a.size * a.dtype.itemsize for a in arrays)
    return pltpu.CompilerParams(vmem_limit_bytes=2 * held + 4 * MIB)


def whole_specs(count):
    return [pl.BlockSpec(memory_space=pltpu.VMEM)] * count


def shape_of(shape, dtype=jnp.float32):
    return jax.ShapeDtypeStruct(shape, dtype)


def prepare_kernel(block_ref, high_ref, low_ref):
    high_ref[...], low_ref[...] = split(block_ref[...].T)


def prepare(block):
    tall, wide = block.shape
    step = min(256, tall)
    out = shape_of((wide, tall), jnp.bfloat16)
    out_spec = pl.BlockSpec((wide, step), lambda i: (0, i))
    return pl.pallas_call(
        prepare_kernel,
        out_shape=(out, out),
        grid=(tall // step,),
        in_specs=[pl.BlockSpec((step, wide), lambda i: (i, 0))],
        out_specs=[out_spec, out_spec],
        compiler_params=pltpu.CompilerParams(vmem_limit_bytes=step * wide * 32 + 4 * MIB),
        cost_estimate=pl.CostEstimate(flops=0, bytes_accessed=block.size * 8, transcendentals=0),
        name="prepare",
    )(block)


def contract_kernel(core, factors_ref, *refs):
    out_ref = refs[-1]
    rows = factors_ref.shape[0]
    parts = []
    for number, high_ref, low_ref in ((core[0], refs[0], refs[1]), (1 - core[0], refs[2], refs[3])):
        wide = high_ref.shape[0]
        high, low = split(factors_ref[:, pl.ds(pl.multiple_of(number * wide, wide), wide)])
        both = jnp.concatenate([high, low], axis=0)
        first = jnp.dot(both, high_ref[...], preferred_element_type=jnp.float32)
        second = jnp.dot(high, low_ref[...], preferred_element_type=jnp.float32)
        parts.append(first[:rows] + (first[rows:] + second))
    out_ref[...] = parts[0] + parts[1]


def contract(core, factors, own, sibling):
    wide, tall = own[0].shape
    out = shape_of((factors.shape[0], tall))
    arrays = [factors, *own, *sibling]
    return pl.pallas_call(
        contract_kernel,
        out_shape=out,
        in_specs=[pl.BlockSpec(memory_space=pltpu.SMEM)] + whole_specs(5),
        out_specs=whole_specs(1)[0],
        compiler_params=params(*arrays, out),
        cost_estimate=pl.CostEstimate(
            flops=12 * out.size * wide, bytes_accessed=own[0].size * 8, transcendentals=0
        ),
        name="contract",
    )(core.reshape(1), *arrays)


def fetch_kernel(x_ref, out_ref):
    out_ref[...] = x_ref[...]


def fetch(x):
    return pl.pallas_call(
        fetch_kernel,
        out_shape=shape_of(x.shape),
        grid=(1,),
        in_specs=[pl.BlockSpec(x.shape, lambda i: (0, 0))],
        out_specs=pl.BlockSpec(memory_space=pltpu.VMEM),
        compiler_params=params(x, x),
        cost_estimate=pl.CostEstimate(flops=0, bytes_accessed=x.size * 8, transcendentals=0),
        name="fetch",
    )(x)


def pick(table, index):
    rows, lanes = table.shape
    length = index.shape[1]
    at_lane = lax.broadcasted_iota(jnp.int32, (lanes, length), 0) == index % lanes
    picked = jnp.dot(
        table,
        at_lane.astype(jnp.float32),
        precision=lax.Precision.HIGHEST,
        preferred_element_type=jnp.float32,
    )
    at_row = lax.broadcasted_iota(jnp.int32, (rows, length), 0) == index // lanes
    return jnp.sum(jnp.where(at_row, picked, 0.0), axis=0, keepdims=True)


def weight_kernel(place, occ_ref, vir_ref, occ_table, vir_table, out_ref):
    energies = []
    for number, length in enumerate(out_ref.shape):
        here = pl.ds(pl.multiple_of(place[number] * length, length), length)
        energies.append(pick(vir_table[...], vir_ref[:, here]) - pick(occ_table[...], occ_ref[:, here]))
    rows, cols = energies
    for start in range(0, out_ref.shape[0], 128):
        column = jnp.broadcast_to(rows[:, start : start + 128], (128, 128)).T
        wide = jnp.concatenate([column] * (out_ref.shape[1] // 128), axis=1)
        out_ref[pl.ds(start, 128), :] = -1.0 / (wide + cols)


def as_table(energies):
    lanes = 128
    padded = jnp.pad(energies, (0, -energies.shape[0] % lanes))
    return padded.reshape(-1, lanes)


def weights(place, occ_index, vir_index, occ_energy, vir_energy, rows, cols):
    occ_index, vir_index = occ_index[None, :], vir_index[None, :]
    occ_table, vir_table = as_table(occ_energy), as_table(vir_energy)
    out = shape_of((rows, cols))
    return pl.pallas_call(
        weight_kernel,
        out_shape=out,
        in_specs=[pl.BlockSpec(memory_space=pltpu.SMEM)] + whole_specs(4),
        out_specs=whole_specs(1)[0],
        compiler_params=pltpu.CompilerParams(vmem_limit_bytes=out.size * 4 + 8 * MIB),
        cost_estimate=pl.CostEstimate(flops=0, bytes_accessed=out.size * 4, transcendentals=0),
        name="weights",
    )(place, occ_index, vir_index, occ_table, vir_table)


def left_kernel(slots, *refs):
    high_ref, low_ref = refs[slots:]
    depth = refs[0].shape[0]
    step = 128 // depth
    for slot in range(0, slots, step):
        block = jnp.concatenate([refs[slot + k][...] for k in range(step)], axis=0).T
        high, low = split(block)
        here = pl.ds(slot * depth, step * depth)
        high_ref[:, here] = high
        low_ref[:, here] = low


def left_parts(left):
    slots = len(left)
    depth, total = left[0].shape
    out = shape_of((total, slots * depth), jnp.bfloat16)
    return pl.pallas_call(
        functools.partial(left_kernel, slots),
        out_shape=(out, out),
        in_specs=whole_specs(slots),
        out_specs=whole_specs(2),
        compiler_params=params(*left, out, out),
        cost_estimate=pl.CostEstimate(flops=0, bytes_accessed=out.size * 8, transcendentals=0),
        name="left_parts",
    )(*left)


CHUNKS = 4


def outer_kernel(spots, depth, place, weights_ref, left_high, left_low, *refs):
    right = refs[: len(spots)]
    out_ref, high_ref, low_ref, result_ref, sems = refs[len(spots) :]
    total, wide = out_ref.shape
    mine = pl.ds(pl.multiple_of(place[0] * wide, wide), wide)
    for ref, (slot, offset) in zip(right, spots):
        high, low = split(ref[:, mine])
        here = pl.ds(pl.multiple_of(place[1 + slot] * depth + offset, ref.shape[0]), ref.shape[0])
        high_ref[here, :] = high
        low_ref[here, :] = low
    tall = total // CHUNKS
    copies = []
    for chunk in range(CHUNKS):
        here = pl.ds(chunk * tall, tall)
        high, low = left_high[here, :], left_low[here, :]
        value = jnp.dot(low, high_ref[...], preferred_element_type=jnp.float32)
        value += jnp.dot(high, low_ref[...], preferred_element_type=jnp.float32)
        value += jnp.dot(high, high_ref[...], preferred_element_type=jnp.float32)
        result_ref[here, :] = value * weights_ref[here, :]
        copies.append(
            pltpu.make_async_copy(result_ref.at[here, :], out_ref.at[here, :], sems.at[chunk])
        )
        copies[-1].start()
    for copy in copies:
        copy.wait()


def outer(place, weights, left_high, left_low, right, spots):
    total, inner = left_high.shape
    depth = right[0].shape[0]
    wide = weights.shape[1]
    arrays = [weights, left_high, left_low, *right]
    out = shape_of((total, wide))
    parts = pltpu.VMEM((inner, wide), jnp.bfloat16)
    return pl.pallas_call(
        functools.partial(outer_kernel, spots, depth),
        out_shape=out,
        in_specs=[pl.BlockSpec(memory_space=pltpu.SMEM)] + whole_specs(len(arrays)),
        out_specs=pl.BlockSpec(memory_space=pl.ANY),
        scratch_shapes=[
            parts,
            parts,
            pltpu.VMEM((total, wide), jnp.float32),
            pltpu.SemaphoreType.DMA((CHUNKS,)),
        ],
        compiler_params=pltpu.CompilerParams(
            vmem_limit_bytes=sum(a.size * a.dtype.itemsize for a in arrays) + out.size * 8 + 8 * MIB
        ),
        cost_estimate=pl.CostEstimate(
            flops=6 * out.size * inner, bytes_accessed=out.size * 4, transcendentals=0
        ),
        name="outer",
    )(place, *arrays)


def local(rows, cols, amplitudes, factors, occ_index, vir_index, occ_energy, vir_energy):
    cores = 2
    share = rows // cores
    chips = [(z, j, s) for z in range(rows) for j in range(rows) for s in range(cores)]

    def number(z, j, s):
        return z * cols + j * cores + s

    def turn(i, s):
        return i if s == 0 else rows - 1 - i

    def move(x, to):
        return lax.ppermute(x, AXES, [(number(*at), number(*to(*at))) for at in chips])

    def swap(x):
        return move(x, lambda z, j, s: (z, j, 1 - s))

    def turned(z, s, i):
        low = z % share ^ i
        return rows - 1 - low if s else low

    def transposed(x, i, swapped=lambda z: z // share):
        def to(z, j, s):
            side, low = divmod(j ^ z, share)
            low = share - 1 - low if side else low
            return (s ^ swapped(z)) * share + (low ^ i), z, side

        return move(x, to)

    def reduced(x, i):
        return move(x, lambda z, j, s: (z, j ^ turned(z, s, i), s))

    def across(x, i):
        return move(x, lambda z, j, s: (z, j ^ turn(i, s), s))

    def within_half(x, v):
        return move(x, lambda z, j, s: (z ^ v, j, s))

    turns = range(share)
    row_index = lax.axis_index("row").astype(jnp.int32)
    col_index = lax.axis_index("col").astype(jnp.int32)
    core = col_index % cores
    tall, wide = amplitudes.shape

    def share_of(x, mine):
        other = swap(x)
        return jnp.where(
            core == 0, jnp.concatenate([mine, other], axis=0), jnp.concatenate([other, mine], axis=0)
        )

    first = jnp.arange(share, dtype=jnp.int32)
    pieces = share_of(factors.T, fetch(factors.T))
    received = [transposed(pieces, i) for i in turns]
    amplitudes, pieces = lax.optimization_barrier((amplitudes, pieces))
    blocks = prepare(amplitudes), prepare(swap(amplitudes))
    partial = [contract(core, x, *blocks) for x in received]
    partial[1], occ_index, vir_index = lax.optimization_barrier((partial[1], occ_index, vir_index))
    arrived = [reduced(partial[i], i) for i in turns]
    factor = weights(
        jnp.stack([row_index, col_index]), occ_index, vir_index, occ_energy, vir_energy, tall, wide
    )
    arrived[1], factor = lax.optimization_barrier((arrived[1], factor))
    total = functools.reduce(jnp.add, arrived)
    total = total + swap(total)
    dressed = pieces + total
    left = [across(dressed, i) for i in turns]
    part = dressed.shape[0] // 2
    right, spots = [transposed(dressed, 0, lambda z: z % 2)], [(0, 0)]
    for v in range(1, share):
        right += [transposed(dressed[part:], v), within_half(right[0][:part], v)]
        spots += [(v, part), (v, 0)]
    spots += [(share + slot, offset) for slot, offset in spots]
    left += [swap(x) for x in left]
    right += [swap(x) for x in right]
    order = jnp.where(core == 0, first, rows - 1 - first)
    order = jnp.concatenate([order, rows - 1 - order])
    low = row_index % share ^ first
    lower, upper = low, rows - 1 - low
    wanted = jnp.concatenate(
        [jnp.where(core == 0, lower, upper), jnp.where(core == 0, upper, lower)]
    )
    at = jnp.sum(
        jnp.where(wanted[:, None] == order[None, :], jnp.arange(rows, dtype=jnp.int32)[None, :], 0), axis=1
    )
    place = jnp.concatenate([core[None], at]).astype(jnp.int32)
    left_high, left_low = left_parts(left)
    return outer(place, factor, left_high, left_low, right, spots)


def solution(mesh):
    rows, cols = mesh.shape["row"], mesh.shape["col"]
    return jax.shard_map(
        functools.partial(local, rows, cols),
        mesh=mesh,
        in_specs=(P("row", "col"), P("row", "col"), P(), P(), P(), P()),
        out_specs=P("row", "col"),
        check_vma=False,
    )
```
